32 devices in a mesh: parts: 2 (over y), aux: 8 (over z, x), pair: 2 (over core).
Axes of the slice: x: 2, y: 2, z: 4, core: 2. Of those that a mesh axis runs over, the one named last changes fastest.
Arguments:
- pair_tensor: float32 [2016, 800], P(('parts', 'aux'), 'pair'), parts along dimension 0, may hold values from -0.625 to 0.625
- occ_energy: float32 [8], P(('parts', 'pair')), parts along dimension 0, may hold values from -1.2 to -0.3
- vir_energy: float32 [400], P('parts'), parts along dimension 0, may hold values from 0.1 to 3
- frequency: float32 [2], P('parts'), parts along dimension 0, may hold values from 0.1 to 4
Outputs:
- response: float32 [2016, 630], P(('parts', 'aux'), 'pair'), parts along dimension 0
The draws below stay inside these ranges and needn't reach their ends.
There are 2 independent parts, one for each index of `parts`. The reference program is written for one: setup_inputs(seed, part) draws one part's arguments, and reference() takes and returns one part's arrays. A program takes and returns all parts, laid end to end along the dimension named above; each array names one. Nothing has to cross between parts.
All inputs are finite; a program needn't handle non-finite values.
Results may differ from the reference program's by a relative error of at most 0.0003.
Values sent between devices are 32-bit elements; how exact they have to be, the bound alone decides.
No kernel may reach another device: no remote copies, remote signals or barrier semaphores. Data moves between devices by JAX's collectives and lax.ppermute only.
A program may use at most 64 MiB of HBM per device.

```python
import math
import jax
import jax.numpy as jnp
from jax import lax

NVIR = 200
AUX_DEV = 126
NAUX = 1008
NOCC = 4
NPAIRS = 800
BLOCKS = 5
KCOLS = 630
N_AUX = 8


def shard_levels(own_key, dims, cuts, smallest, top_value):
    def one(dim, shards_of):
        heights = jax.random.uniform(jax.random.fold_in(jax.random.fold_in(own_key, 6), dim), (shards_of,), jnp.float32, smallest / len(cuts), top_value / len(cuts))
        return jnp.repeat(jnp.exp(heights), dims[dim] // shards_of).reshape((-1,) + (1,) * (len(dims) - dim - 1))

    factor_of = one(*cuts[0])
    for cut in cuts[1:]:
        factor_of = factor_of * one(*cut)
    return factor_of


def bell_draw(own_key, dims, width, limit, shards=(), kind=jnp.bfloat16):
    loudness = shard_levels(own_key, dims, shards, -0.22, 0.18) if shards else 1.0
    values = jax.random.normal(own_key, dims, jnp.float32) * width * loudness
    return jnp.minimum(jnp.maximum(values, -limit), limit).astype(kind)


def setup_inputs(seed: int = 0, part: int = 0) -> dict:
    seeds = jax.random.split(jax.random.key(seed), 5)
    own_keys = jax.random.split(jax.random.fold_in(seeds[4], part), 5)
    return {
        "pair_tensor": bell_draw(own_keys[0], (NAUX, NPAIRS), 0.1, 0.625, ((0, 8), (1, 2)), jnp.float32),
        "occ_energy": jnp.clip(-1.2 + 0.90000004 * jax.random.uniform(own_keys[1], (NOCC,), jnp.float32) ** shard_levels(own_keys[1], (NOCC,), ((0, 2),), -0.2, 0.2), -1.2, -0.3),
        "vir_energy": jnp.clip(jax.random.uniform(own_keys[2], (NVIR,), jnp.float32, 0.1, 3.0), 0.1, 3.0),
        "frequency": jnp.clip(jnp.exp(jax.random.uniform(own_keys[3], (1,), jnp.float32, math.log(0.1), math.log(4.0))), 0.1, 4.0),
    }


def pair_weights(occ_energy, vir_energy, frequency):
    energy_gap = vir_energy[None, :] - occ_energy[:, None]
    return (4.0 * energy_gap / (energy_gap * energy_gap + frequency[0] * frequency[0])).reshape(-1)


def reference(pair_tensor, occ_energy, vir_energy, frequency):
    weights = pair_weights(occ_energy, vir_energy, frequency)
    blocks = pair_tensor.reshape(N_AUX, AUX_DEV, pair_tensor.shape[1])
    offsets = jnp.arange(BLOCKS, dtype=jnp.int32)

    def row_block(block_index):
        own_rows = blocks[block_index] * weights[None, :]
        chosen = jnp.take(blocks, (block_index + offsets) % N_AUX, axis=0).reshape(KCOLS, pair_tensor.shape[1])
        return lax.dot_general(own_rows, chosen, (((1,), (1,)), ((), ())), precision=lax.Precision.HIGHEST, preferred_element_type=jnp.float32)

    row_tiles = lax.map(row_block, jnp.arange(N_AUX, dtype=jnp.int32))
    return row_tiles.reshape(NAUX, KCOLS)
```

```python
import jax
import jax.numpy as jnp
from jax import lax
from jax.experimental import pallas as pl
from jax.experimental.pallas import tpu as pltpu
from jax.sharding import PartitionSpec as P


def passed_along(value, axis, by):
    peers = lax.axis_size(axis)
    return lax.ppermute(value, axis, [(i, (i + by) % peers) for i in range(peers)])


def pair_weights(occ_energy, vir_energy, frequency):
    energy_gap = vir_energy[None, :] - occ_energy[:, None]
    return (4.0 * energy_gap / (energy_gap * energy_gap + frequency[0] * frequency[0])).reshape(-1)


def product_tile(scaled_rows, block_rows):
    return lax.dot_general(
        scaled_rows,
        block_rows,
        (((1,), (1,)), ((), ())),
        precision=lax.Precision.HIGHEST,
        preferred_element_type=jnp.float32,
    )


def write_block(collected, values, column):
    return lax.dynamic_update_slice_in_dim(collected, values, column, 1)


def half_turn(scaled_rows, first_block, half_span):
    row_count = scaled_rows.shape[0]
    collected = jnp.zeros((row_count, (half_span + 1) * row_count), jnp.float32)
    collected = write_block(collected, product_tile(scaled_rows, first_block), 0)
    opposite = passed_along(first_block, "aux", -half_span)
    collected = write_block(collected, product_tile(scaled_rows, opposite), half_span * row_count)

    def advance(turn_index, loop_state):
        collected, forward, backward = loop_state
        forward = passed_along(forward, "aux", -1)
        backward = passed_along(backward, "aux", 1)
        collected = write_block(
            collected, product_tile(scaled_rows, forward), turn_index * row_count
        )
        collected = write_block(
            collected, product_tile(scaled_rows, backward), (half_span - turn_index) * row_count
        )
        return (collected, forward, backward)

    collected, forward, backward = lax.fori_loop(
        1, half_span // 2, advance, (collected, first_block, opposite)
    )
    middle = passed_along(forward, "aux", -1)
    return write_block(collected, product_tile(scaled_rows, middle), half_span // 2 * row_count)


def ring_shards(pair_tensor, occ_energy, vir_energy, frequency):
    n_aux = lax.axis_size("aux")
    scaled_rows = pair_tensor * pair_weights(occ_energy, vir_energy, frequency)[None, :]
    collected = half_turn(scaled_rows, pair_tensor, n_aux // 2)
    return lax.psum_scatter(collected, "pair", scatter_dimension=1, tiled=True)


def sent(value, target_of):
    pairs = []
    for z in range(4):
        for x in range(2):
            for c in range(2):
                target = target_of(z, x, c)
                if target is not None:
                    tz, tx, tc = target
                    pairs.append(((z * 2 + x) * 2 + c, (tz * 2 + tx) * 2 + tc))
    return lax.ppermute(value, ("aux", "pair"), pairs)


def to_other_core(z, x, c):
    return (z, x, 1 - c)


def far_of_odd_xp_of_even(z, x, c):
    return (z ^ 2, x, c) if z % 2 else (z, 1 - x, c)


def far_of_even_xp_of_odd(z, x, c):
    return (z, 1 - x, c) if z % 2 else (z ^ 2, 1 - x, c)


def neighbour(z, x, c):
    return (z ^ 1, x, c)


def early_tile(z, x, c):
    if z % 2:
        return (z ^ 2, x, c)
    return (z, 1 - x, c) if x == c else None


def late_tile(z, x, c):
    if z % 2:
        return (z, 1, 1) if (x, c) == (0, 1) else None
    return (z, 1 - x, 1) if x == c else (z ^ 1, x, 1 - x)


def place():
    block = lax.axis_index("aux")
    return lax.rem(block // 2, 2) == 0, lax.rem(block, 2), lax.axis_index("pair")


def halves(value):
    high = value.astype(jnp.bfloat16)
    return high, (value - high.astype(jnp.float32)).astype(jnp.bfloat16)


def summed_over_pairs(left, right):
    left_high, left_low = left
    right_high, right_low = right
    return lax.dot_general(
        jnp.concatenate([left_high, left_low, left_high], 0),
        jnp.concatenate([right_high, right_high, right_low], 0),
        (((0,), (0,)), ((), ())),
        preferred_element_type=jnp.float32,
    )


def tile_of(left_blocks, right_blocks):
    total = None
    for left, right in zip(left_blocks, right_blocks):
        part = summed_over_pairs(halves(left), halves(right))
        total = part if total is None else total + part
    return total


def early_kernel(weight, weight2, zn, zn2, a, a2, tile):
    tile[...] = tile_of(
        (zn[...], zn2[...]), (a[...] * weight[...], a2[...] * weight2[...])
    )


def local_kernel(weight, weight2, own, own2, zn, zn2, a, a2, own_own, a_own, zn_own):
    scaled = (own[...] * weight[...], own2[...] * weight2[...])
    own_own[...] = tile_of((own[...], own2[...]), scaled)
    a_own[...] = tile_of((a[...], a2[...]), scaled)
    zn_own[...] = tile_of((zn[...], zn2[...]), scaled)


def late_kernel(weight, weight2, zn, zn2, a, a2, b, b2, tile):
    even, x, c = place()
    b_blocks = (b[...], b2[...])

    @pl.when(even & (x == c))
    def _():
        tile[...] = tile_of(b_blocks, (a[...] * weight[...], a2[...] * weight2[...]))

    @pl.when(even & (x != c))
    def _():
        tile[...] = tile_of(b_blocks, (zn[...] * weight[...], zn2[...] * weight2[...]))

    @pl.when(~even)
    def _():
        tile[...] = tile_of((a[...] * weight[...], a2[...] * weight2[...]), b_blocks)


def gather_kernel(weight, weight2, own, own2, b, b2, own_own, a_own, zn_own, early, kept):
    even, x, c = place()
    rows = own_own.shape[0]
    half = rows // 2

    @pl.when(c == 0)
    def _():
        kept[pl.ds(0, rows), :] = own_own[...]

        @pl.when(even & (x == 0))
        def _():
            kept[pl.ds(rows, rows), :] = a_own[...]

        @pl.when(even & (x == 1))
        def _():
            kept[pl.ds(rows, rows), :] = early[...]

        @pl.when(~even)
        def _():
            kept[pl.ds(rows, rows), :] = tile_of(
                (b[...], b2[...]), (own[...] * weight[...], own2[...] * weight2[...])
            )

        @pl.when(even)
        def _():
            kept[pl.ds(2 * rows, half), :] = zn_own[pl.ds(0, half), :]

        @pl.when(~even)
        def _():
            kept[pl.ds(2 * rows, half), :] = early[pl.ds(0, half), :]

    @pl.when(c == 1)
    def _():
        @pl.when(even)
        def _():
            kept[pl.ds(0, half), :] = zn_own[pl.ds(half, half), :]

        @pl.when(~even)
        def _():
            kept[pl.ds(0, half), :] = early[pl.ds(half, half), :]

        @pl.when(even & (x == 0))
        def _():
            kept[pl.ds(half, rows), :] = early[...]

        @pl.when(even & (x == 1))
        def _():
            kept[pl.ds(half, rows), :] = tile_of(
                (b[...], b2[...]), (own[...] * weight[...], own2[...] * weight2[...])
            )

        @pl.when(~even)
        def _():
            kept[pl.ds(half, rows), :] = a_own[...]

        kept[pl.ds(half + rows, rows), :] = a_own[...]


def finish_kernel(kept, late, response):
    even, x, c = place()
    rows = late.shape[0]
    half = rows // 2
    response[...] = kept[...]

    @pl.when((c == 0) & ~even & (x == 1))
    def _():
        response[pl.ds(rows, rows), :] = late[...]

    @pl.when((c == 1) & even)
    def _():
        response[pl.ds(half + rows, rows), :] = late[...]

    @pl.when((c == 1) & ~even)
    def _():
        response[pl.ds(half, rows), :] = late[...]


def in_vmem(kernel, shapes, *operands):
    whole = pl.BlockSpec(memory_space=pltpu.VMEM)
    out_shape = [jax.ShapeDtypeStruct(shape, jnp.float32) for shape in shapes]
    return pl.pallas_call(
        kernel,
        out_shape=out_shape,
        in_specs=[whole] * len(operands),
        out_specs=[whole] * len(shapes),
        compiler_params=pltpu.CompilerParams(vmem_limit_bytes=32 * 1024 * 1024),
    )(*operands)


def octet_shards(pair_tensor, occ_energy, vir_energy, frequency):
    own = pair_tensor.T
    pairs, rows = own.shape
    a = sent(own, far_of_odd_xp_of_even)
    b = sent(own, far_of_even_xp_of_odd)
    zn = sent(own, neighbour)
    own2 = sent(own, to_other_core)
    occ_energy2 = sent(occ_energy, to_other_core)
    weight, weight2 = (
        jnp.broadcast_to(pair_weights(e, vir_energy, frequency)[:, None], (pairs, rows))
        for e in (occ_energy, occ_energy2)
    )
    weights = (weight, weight2)
    a_both = (a, sent(a, to_other_core))
    zn_both = (zn, sent(zn, to_other_core))
    square = (rows, rows)
    (early,) = in_vmem(early_kernel, [square], *weights, *zn_both, *a_both)
    early = sent(early, early_tile)
    own_own, a_own, zn_own = in_vmem(
        local_kernel, [square] * 3, *weights, own, own2, *zn_both, *a_both
    )
    b_both = (b, sent(b, to_other_core))
    (late,) = in_vmem(late_kernel, [square], *weights, *zn_both, *a_both, *b_both)
    late = sent(late, late_tile)
    kept_shape = (5 * rows // 2, rows)
    (kept,) = in_vmem(
        gather_kernel, [kept_shape], *weights, own, own2, *b_both, own_own, a_own, zn_own, early
    )
    (response,) = in_vmem(finish_kernel, [kept_shape], kept, late)
    return response.T


def solution(mesh):
    in_specs = (P(("parts", "aux"), "pair"), P(("parts", "pair")), P("parts"), P("parts"))
    out_specs = P(("parts", "aux"), "pair")
    octet = mesh.shape["aux"] == 8 and mesh.shape["pair"] == 2
    shards = octet_shards if octet else ring_shards
    return jax.shard_map(shards, mesh=mesh, in_specs=in_specs, out_specs=out_specs, check_vma=False)
```

```python
import jax
import jax.numpy as jnp
from jax import lax
from jax.experimental import pallas as pl
from jax.experimental.pallas import tpu as pltpu
from jax.sharding import PartitionSpec as P


def passed_along(value, axis, by):
    peers = lax.axis_size(axis)
    return lax.ppermute(value, axis, [(i, (i + by) % peers) for i in range(peers)])


def pair_weights(occ_energy, vir_energy, frequency):
    energy_gap = vir_energy[None, :] - occ_energy[:, None]
    return (4.0 * energy_gap / (energy_gap * energy_gap + frequency[0] * frequency[0])).reshape(-1)


def product_tile(scaled_rows, block_rows):
    return lax.dot_general(
        scaled_rows,
        block_rows,
        (((1,), (1,)), ((), ())),
        precision=lax.Precision.HIGHEST,
        preferred_element_type=jnp.float32,
    )


def write_block(collected, values, column):
    return lax.dynamic_update_slice_in_dim(collected, values, column, 1)


def half_turn(scaled_rows, first_block, half_span):
    row_count = scaled_rows.shape[0]
    collected = jnp.zeros((row_count, (half_span + 1) * row_count), jnp.float32)
    collected = write_block(collected, product_tile(scaled_rows, first_block), 0)
    opposite = passed_along(first_block, "aux", -half_span)
    collected = write_block(collected, product_tile(scaled_rows, opposite), half_span * row_count)

    def advance(turn_index, loop_state):
        collected, forward, backward = loop_state
        forward = passed_along(forward, "aux", -1)
        backward = passed_along(backward, "aux", 1)
        collected = write_block(
            collected, product_tile(scaled_rows, forward), turn_index * row_count
        )
        collected = write_block(
            collected, product_tile(scaled_rows, backward), (half_span - turn_index) * row_count
        )
        return (collected, forward, backward)

    collected, forward, backward = lax.fori_loop(
        1, half_span // 2, advance, (collected, first_block, opposite)
    )
    middle = passed_along(forward, "aux", -1)
    return write_block(collected, product_tile(scaled_rows, middle), half_span // 2 * row_count)


def ring_shards(pair_tensor, occ_energy, vir_energy, frequency):
    n_aux = lax.axis_size("aux")
    scaled_rows = pair_tensor * pair_weights(occ_energy, vir_energy, frequency)[None, :]
    collected = half_turn(scaled_rows, pair_tensor, n_aux // 2)
    return lax.psum_scatter(collected, "pair", scatter_dimension=1, tiled=True)


def sent(value, target_of):
    pairs = []
    for z in range(4):
        for x in range(2):
            for c in range(2):
                tz, tx, tc = target_of(z, x, c)
                pairs.append(((z * 2 + x) * 2 + c, (tz * 2 + tx) * 2 + tc))
    return lax.ppermute(value, ("aux", "pair"), pairs)


def other_core(z, x, c):
    return (z, x, 1 - c)


def far_chip(z, x, c):
    return (z ^ 2, x, c)


def other_x(z, x, c):
    return (z, 1 - x, c)


def next_chip(z, x, c):
    return (z ^ 1, x if z % 2 else 1 - x, c)


def tile_chip(z, x, c):
    if z % 2 == 0:
        return (z, 1 - x, c)
    return (z ^ 2, x, c) if x != c else (z, 1 - x, 1 - c)


def half_tile_chip(z, x, c):
    return (z ^ 1, x, c)


def place():
    block = lax.axis_index("aux")
    return lax.rem(block // 2, 2) == 0, lax.rem(block, 2), lax.axis_index("pair")


def halves(value):
    high = value.astype(jnp.bfloat16)
    return high, (value - high.astype(jnp.float32)).astype(jnp.bfloat16)


def summed_over_pairs(left, right):
    left_high, left_low = left
    right_high, right_low = right
    return lax.dot_general(
        jnp.concatenate([left_high, left_low, left_high], 0),
        jnp.concatenate([right_high, right_high, right_low], 0),
        (((0,), (0,)), ((), ())),
        preferred_element_type=jnp.float32,
    )


def tile_of(left_blocks, right_blocks):
    total = None
    for left, right in zip(left_blocks, right_blocks):
        part = summed_over_pairs(halves(left), halves(right))
        total = part if total is None else total + part
    return total


def scale_kernel(weight, weight2, xp, xp2, zn, zn2, xp_scaled, zn_scaled):
    xp_scaled[0] = xp[...] * weight[...]
    xp_scaled[1] = xp2[...] * weight2[...]
    zn_scaled[0] = zn[...] * weight[...]
    zn_scaled[1] = zn2[...] * weight2[...]


def tile_kernel(zn, zn2, xp_scaled, zn_scaled, far, far2, tile):
    even, x, c = place()
    far_blocks = (far[...], far2[...])

    def far_xp():
        tile[...] = tile_of(far_blocks, (xp_scaled[0], xp_scaled[1]))

    @pl.when(even & (x == 0) & (c == 1))
    def _():
        far_xp()

    @pl.when(~even & (x == 0) & (c == 0))
    def _():
        far_xp()

    @pl.when(even & ((x == 1) | (c == 0)))
    def _():
        tile[...] = tile_of((zn[...], zn2[...]), (xp_scaled[0], xp_scaled[1]))

    @pl.when(~even & ((x == 1) | (c == 1)))
    def _():
        tile[...] = tile_of((zn_scaled[0], zn_scaled[1]), far_blocks)


def half_tile_kernel(zn_scaled, far, far2, half_tile):
    _, _, c = place()
    half = half_tile.shape[0]
    tile = tile_of((far[...], far2[...]), (zn_scaled[0], zn_scaled[1]))

    @pl.when(c == 0)
    def _():
        half_tile[...] = tile[:half]

    @pl.when(c == 1)
    def _():
        half_tile[...] = tile[half:]


def local_kernel(weight, weight2, own, own2, xp, xp2, zn, zn2, far, far2, kept):
    even, x, c = place()
    rows = own.shape[1]
    half = rows // 2
    scaled = (own[...] * weight[...], own2[...] * weight2[...])

    @pl.when(c == 0)
    def _():
        kept[pl.ds(0, rows), :] = tile_of((own[...], own2[...]), scaled)
        kept[pl.ds(rows, rows), :] = tile_of((xp[...], xp2[...]), scaled)

    @pl.when(c == 1)
    def _():
        kept[pl.ds(half, rows), :] = jnp.zeros((rows, rows), jnp.float32)
        kept[pl.ds(half + rows, rows), :] = tile_of((far[...], far2[...]), scaled)

    zn_own = tile_of((zn[...], zn2[...]), scaled)

    @pl.when(c == 0)
    def _():
        kept[pl.ds(2 * rows, half), :] = zn_own[:half]

    @pl.when(c == 1)
    def _():
        kept[pl.ds(0, half), :] = zn_own[half:]


def finish_kernel(kept, tile, half_tile, response):
    even, x, c = place()
    rows = tile.shape[0]
    half = rows // 2
    response[...] = kept[...]

    @pl.when((c == 0) & (x == 1))
    def _():
        response[pl.ds(rows, rows), :] = tile[...]

    @pl.when(c == 1)
    def _():
        response[pl.ds(half, rows), :] = tile[...]

    @pl.when((c == 0) & ~even)
    def _():
        response[pl.ds(2 * rows, half), :] = half_tile[...]

    @pl.when((c == 1) & ~even)
    def _():
        response[pl.ds(0, half), :] = half_tile[...]


def in_vmem(kernel, shapes, *operands):
    whole = pl.BlockSpec(memory_space=pltpu.VMEM)
    out_shape = [jax.ShapeDtypeStruct(shape, jnp.float32) for shape in shapes]
    return pl.pallas_call(
        kernel,
        out_shape=out_shape,
        in_specs=[whole] * len(operands),
        out_specs=[whole] * len(shapes),
        compiler_params=pltpu.CompilerParams(vmem_limit_bytes=32 * 1024 * 1024),
        cost_estimate=pl.CostEstimate(flops=1000, bytes_accessed=1000, transcendentals=0),
    )(*operands)


def octet_shards(pair_tensor, occ_energy, vir_energy, frequency):
    own = pair_tensor.T
    pairs, rows = own.shape
    far = sent(own, far_chip)
    xp = sent(own, other_x)
    zn = sent(own, next_chip)
    own2 = sent(own, other_core)
    occ_energy2 = sent(occ_energy, other_core)
    weights = tuple(
        jnp.broadcast_to(pair_weights(e, vir_energy, frequency)[:, None], (pairs, rows))
        for e in (occ_energy, occ_energy2)
    )
    far2, xp2, zn2 = (sent(v, other_core) for v in (far, xp, zn))
    xp_scaled, zn_scaled = in_vmem(
        scale_kernel, [(2, pairs, rows)] * 2, *weights, xp, xp2, zn, zn2
    )
    (tile,) = in_vmem(
        tile_kernel, [(rows, rows)], zn, zn2, xp_scaled, zn_scaled, far, far2
    )
    tile = sent(tile, tile_chip)
    (half_tile,) = in_vmem(half_tile_kernel, [(rows // 2, rows)], zn_scaled, far, far2)
    half_tile = sent(half_tile, half_tile_chip)
    kept_shape = (5 * rows // 2, rows)
    (kept,) = in_vmem(
        local_kernel, [kept_shape], *weights, own, own2, xp, xp2, zn, zn2, far, far2
    )
    (response,) = in_vmem(finish_kernel, [kept_shape], kept, tile, half_tile)
    return response.T


def solution(mesh):
    in_specs = (P(("parts", "aux"), "pair"), P(("parts", "pair")), P("parts"), P("parts"))
    out_specs = P(("parts", "aux"), "pair")
    octet = mesh.shape["aux"] == 8 and mesh.shape["pair"] == 2
    shards = octet_shards if octet else ring_shards
    return jax.shard_map(shards, mesh=mesh, in_specs=in_specs, out_specs=out_specs, check_vma=False)
```

```python
import functools

import jax
import jax.numpy as jnp
from jax import lax
from jax.experimental import pallas as pl
from jax.experimental.pallas import tpu as pltpu
from jax.sharding import PartitionSpec as P


def passed_along(value, axis, by):
    peers = lax.axis_size(axis)
    return lax.ppermute(value, axis, [(i, (i + by) % peers) for i in range(peers)])


def pair_weights(occ_energy, vir_energy, frequency):
    energy_gap = vir_energy[None, :] - occ_energy[:, None]
    return (4.0 * energy_gap / (energy_gap * energy_gap + frequency[0] * frequency[0])).reshape(-1)


def product_tile(scaled_rows, block_rows):
    return lax.dot_general(
        scaled_rows,
        block_rows,
        (((1,), (1,)), ((), ())),
        precision=lax.Precision.HIGHEST,
        preferred_element_type=jnp.float32,
    )


def write_block(collected, values, column):
    return lax.dynamic_update_slice_in_dim(collected, values, column, 1)


def half_turn(scaled_rows, first_block, half_span):
    row_count = scaled_rows.shape[0]
    collected = jnp.zeros((row_count, (half_span + 1) * row_count), jnp.float32)
    collected = write_block(collected, product_tile(scaled_rows, first_block), 0)
    opposite = passed_along(first_block, "aux", -half_span)
    collected = write_block(collected, product_tile(scaled_rows, opposite), half_span * row_count)

    def advance(turn_index, loop_state):
        collected, forward, backward = loop_state
        forward = passed_along(forward, "aux", -1)
        backward = passed_along(backward, "aux", 1)
        collected = write_block(
            collected, product_tile(scaled_rows, forward), turn_index * row_count
        )
        collected = write_block(
            collected, product_tile(scaled_rows, backward), (half_span - turn_index) * row_count
        )
        return (collected, forward, backward)

    collected, forward, backward = lax.fori_loop(
        1, half_span // 2, advance, (collected, first_block, opposite)
    )
    middle = passed_along(forward, "aux", -1)
    return write_block(collected, product_tile(scaled_rows, middle), half_span // 2 * row_count)


def ring_shards(pair_tensor, occ_energy, vir_energy, frequency):
    n_aux = lax.axis_size("aux")
    scaled_rows = pair_tensor * pair_weights(occ_energy, vir_energy, frequency)[None, :]
    collected = half_turn(scaled_rows, pair_tensor, n_aux // 2)
    return lax.psum_scatter(collected, "pair", scatter_dimension=1, tiled=True)


def sent(value, target_of):
    pairs = []
    for z in range(4):
        for x in range(2):
            for c in range(2):
                tz, tx, tc = target_of(z, x, c)
                pairs.append(((z * 2 + x) * 2 + c, (tz * 2 + tx) * 2 + tc))
    return lax.ppermute(value, ("aux", "pair"), pairs)


def other_core(z, x, c):
    return (z, x, 1 - c)


def far_chip(z, x, c):
    return (z ^ 2, x, c)


def other_x(z, x, c):
    return (z, 1 - x, c)


def next_chip(z, x, c):
    return (z ^ 1, x if z % 2 else 1 - x, c)


def tile_chip(z, x, c):
    if z % 2 == 0:
        return (z, 1 - x, c)
    return (z ^ 2, x, c) if x != c else (z, 1 - x, 1 - c)


def half_tile_chip(z, x, c):
    return (z ^ 1, x, c)


def place():
    block = lax.axis_index("aux")
    return lax.rem(block // 2, 2) == 0, lax.rem(block, 2), lax.axis_index("pair")


def halves(value):
    high = value.astype(jnp.bfloat16)
    return high, (value - high.astype(jnp.float32)).astype(jnp.bfloat16)


def stack_kernel(order, block, stack):
    pairs, rows = block.shape
    parts = halves(block[...])
    for i, part in enumerate(order):
        stack[pl.ds(i * pairs, pairs), pl.ds(0, rows)] = parts[part]


def scaled_kernel(weight, block, stack):
    pairs, rows = block.shape
    parts = halves(block[...] * weight[...])
    for i, part in enumerate((0, 0, 1)):
        stack[pl.ds(i * pairs, pairs), pl.ds(0, rows)] = parts[part]


def meet_kernel(far, xp, xp_scaled, zn_scaled, mine, theirs):
    even, x, c = place()
    rows = mine.shape[1]
    half = rows // 2
    tiles = lax.dot_general(
        jnp.concatenate([far[...], xp[...]], 1),
        jnp.concatenate([zn_scaled[...], xp_scaled[...]], 1),
        (((0,), (0,)), ((), ())),
        preferred_element_type=jnp.float32,
    )
    far_zn, far_xp = tiles[:rows, :rows], tiles[:rows, 128 : 128 + rows]
    xp_zn = tiles[128 : 128 + rows, :rows]

    def put(core, row, values):
        @pl.when(c == core)
        def _():
            mine[pl.ds(row, values.shape[0]), :] = values

        @pl.when(c != core)
        def _():
            theirs[pl.ds(row, values.shape[0]), :] = values

    put(0, rows, far_zn[:half])
    put(1, rows, far_zn[half:])

    @pl.when(even)
    def _():
        zn_xp = xp_zn.T
        put(0, 0, zn_xp)

        @pl.when(x == 0)
        def _():
            put(1, 0, far_xp)

        @pl.when(x == 1)
        def _():
            put(1, 0, zn_xp)

    @pl.when(~even)
    def _():
        zn_far = far_zn.T
        put(1, 0, zn_far)

        @pl.when(x == 0)
        def _():
            put(0, 0, far_xp)

        @pl.when(x == 1)
        def _():
            put(0, 0, zn_far)


def sum_kernel(mine, theirs, tile, half_tile):
    rows, half = tile.shape[0], half_tile.shape[0]
    tile[...] = mine[pl.ds(0, rows), :] + theirs[pl.ds(0, rows), :]
    half_tile[...] = mine[pl.ds(rows, half), :] + theirs[pl.ds(rows, half), :]


def dot_over_pairs(left, right):
    return lax.dot_general(
        left, right, (((0,), (0,)), ((), ())), preferred_element_type=jnp.float32
    )


def local_kernel(own, own_scaled, xp, zn_scaled, mine, theirs):
    even, x, c = place()
    rows = mine.shape[1]
    half = rows // 2
    own_stack = own[...]
    by_own = dot_over_pairs(jnp.concatenate([own_stack, xp[...]], 1), own_scaled[...])
    own_own, xp_own = by_own[:rows, :rows], by_own[128 : 128 + rows, :rows]
    zn_own = dot_over_pairs(zn_scaled[...], own_stack)[:rows, :rows]

    def first(kept):
        kept[pl.ds(0, rows), :] = own_own
        kept[pl.ds(rows, rows), :] = xp_own
        kept[pl.ds(2 * rows, half), :] = zn_own[:half]

    def second(kept):
        kept[pl.ds(0, half), :] = zn_own[half:]
        kept[pl.ds(half, 2 * rows), :] = jnp.zeros((2 * rows, rows), jnp.float32)

    @pl.when(c == 0)
    def _():
        first(mine)
        second(theirs)

    @pl.when(c == 1)
    def _():
        first(theirs)
        second(mine)


def far_kernel(weight, own, far, far_own):
    far_own[...] = tile_of(far[...], own[...] * weight[...])


def far_kernel(far, own_scaled, far_own):
    rows = far_own.shape[0]
    far_own[...] = dot_over_pairs(far[...], own_scaled[...])[:rows, :rows]


def finish_kernel(mine, theirs, far_own, far_own2, tile, half_tile, response):
    even, x, c = place()
    rows = tile.shape[0]
    half = rows // 2
    response[...] = mine[...] + theirs[...]

    @pl.when((c == 0) & (x == 1))
    def _():
        response[pl.ds(rows, rows), :] = tile[...]

    @pl.when(c == 1)
    def _():
        response[pl.ds(half, rows), :] = tile[...]
        response[pl.ds(half + rows, rows), :] = far_own[...] + far_own2[...]

    @pl.when((c == 0) & ~even)
    def _():
        response[pl.ds(2 * rows, half), :] = half_tile[...]

    @pl.when((c == 1) & ~even)
    def _():
        response[pl.ds(0, half), :] = half_tile[...]


def in_vmem(kernel, outs, *operands, flops=1000):
    whole = pl.BlockSpec(memory_space=pltpu.VMEM)
    return pl.pallas_call(
        kernel,
        out_shape=[jax.ShapeDtypeStruct(*out) for out in outs],
        in_specs=[whole] * len(operands),
        out_specs=[whole] * len(outs),
        compiler_params=pltpu.CompilerParams(vmem_limit_bytes=32 * 1024 * 1024),
        cost_estimate=pl.CostEstimate(flops=flops, bytes_accessed=1000, transcendentals=0),
    )(*operands)


def octet_shards(pair_tensor, occ_energy, vir_energy, frequency):
    own = pair_tensor.T
    pairs, rows = own.shape
    weight = jnp.broadcast_to(
        pair_weights(occ_energy, vir_energy, frequency)[:, None], (pairs, rows)
    )
    stack = ((3 * pairs, 128), jnp.bfloat16)
    plain = functools.partial(stack_kernel, (0, 1, 0))
    far = sent(own, far_chip)
    xp = sent(own, other_x)
    zn = sent(own, next_chip)
    (far_stack,) = in_vmem(plain, [stack], far, flops=10**11)
    (zn_scaled,) = in_vmem(scaled_kernel, [stack], weight, zn)
    xp, zn_scaled = lax.optimization_barrier((xp, zn_scaled))
    (xp_stack,) = in_vmem(plain, [stack], xp)
    (xp_scaled,) = in_vmem(scaled_kernel, [stack], weight, xp)
    parts = ((3 * rows // 2, rows), jnp.float32)
    mine, theirs = in_vmem(
        meet_kernel, [parts] * 2, far_stack, xp_stack, xp_scaled, zn_scaled
    )
    square, half_square = ((rows, rows), jnp.float32), ((rows // 2, rows), jnp.float32)
    tile, half_tile = in_vmem(
        sum_kernel, [square, half_square], mine, sent(theirs, other_core)
    )
    tile = sent(tile, tile_chip)
    half_tile = sent(half_tile, half_tile_chip)
    (own_stack,) = in_vmem(plain, [stack], own)
    (own_scaled,) = in_vmem(scaled_kernel, [stack], weight, own)
    kept = ((5 * rows // 2, rows), jnp.float32)
    mine, theirs = in_vmem(
        local_kernel, [kept] * 2, own_stack, own_scaled, xp_stack, zn_scaled
    )
    (far_own,) = in_vmem(far_kernel, [square], far_stack, own_scaled)
    (response,) = in_vmem(
        finish_kernel,
        [kept],
        mine,
        sent(theirs, other_core),
        far_own,
        sent(far_own, other_core),
        tile,
        half_tile,
    )
    return response.T


def solution(mesh):
    in_specs = (P(("parts", "aux"), "pair"), P(("parts", "pair")), P("parts"), P("parts"))
    out_specs = P(("parts", "aux"), "pair")
    octet = mesh.shape["aux"] == 8 and mesh.shape["pair"] == 2
    shards = octet_shards if octet else ring_shards
    return jax.shard_map(shards, mesh=mesh, in_specs=in_specs, out_specs=out_specs, check_vma=False)
```

```python
import functools

import jax
import jax.numpy as jnp
from jax import lax
from jax.experimental import pallas as pl
from jax.experimental.pallas import tpu as pltpu
from jax.sharding import PartitionSpec as P


def passed_along(value, axis, by):
    peers = lax.axis_size(axis)
    return lax.ppermute(value, axis, [(i, (i + by) % peers) for i in range(peers)])


def pair_weights(occ_energy, vir_energy, frequency):
    energy_gap = vir_energy[None, :] - occ_energy[:, None]
    return (4.0 * energy_gap / (energy_gap * energy_gap + frequency[0] * frequency[0])).reshape(-1)


def product_tile(scaled_rows, block_rows):
    return lax.dot_general(
        scaled_rows,
        block_rows,
        (((1,), (1,)), ((), ())),
        precision=lax.Precision.HIGHEST,
        preferred_element_type=jnp.float32,
    )


def write_block(collected, values, column):
    return lax.dynamic_update_slice_in_dim(collected, values, column, 1)


def half_turn(scaled_rows, first_block, half_span):
    row_count = scaled_rows.shape[0]
    collected = jnp.zeros((row_count, (half_span + 1) * row_count), jnp.float32)
    collected = write_block(collected, product_tile(scaled_rows, first_block), 0)
    opposite = passed_along(first_block, "aux", -half_span)
    collected = write_block(collected, product_tile(scaled_rows, opposite), half_span * row_count)

    def advance(turn_index, loop_state):
        collected, forward, backward = loop_state
        forward = passed_along(forward, "aux", -1)
        backward = passed_along(backward, "aux", 1)
        collected = write_block(
            collected, product_tile(scaled_rows, forward), turn_index * row_count
        )
        collected = write_block(
            collected, product_tile(scaled_rows, backward), (half_span - turn_index) * row_count
        )
        return (collected, forward, backward)

    collected, forward, backward = lax.fori_loop(
        1, half_span // 2, advance, (collected, first_block, opposite)
    )
    middle = passed_along(forward, "aux", -1)
    return write_block(collected, product_tile(scaled_rows, middle), half_span // 2 * row_count)


def ring_shards(pair_tensor, occ_energy, vir_energy, frequency):
    n_aux = lax.axis_size("aux")
    scaled_rows = pair_tensor * pair_weights(occ_energy, vir_energy, frequency)[None, :]
    collected = half_turn(scaled_rows, pair_tensor, n_aux // 2)
    return lax.psum_scatter(collected, "pair", scatter_dimension=1, tiled=True)


def sent(value, target_of):
    pairs = []
    for z in range(4):
        for x in range(2):
            for c in range(2):
                tz, tx, tc = target_of(z, x, c)
                pairs.append(((z * 2 + x) * 2 + c, (tz * 2 + tx) * 2 + tc))
    return lax.ppermute(value, ("aux", "pair"), pairs)


def other_core(z, x, c):
    return (z, x, 1 - c)


def far_chip(z, x, c):
    return (z ^ 2, x, c)


def other_x(z, x, c):
    return (z, 1 - x, c)


def next_chip(z, x, c):
    return (z ^ 1, x if z % 2 else 1 - x, c)


def tile_chip(z, x, c):
    if z % 2 == 0:
        return (z, 1 - x, c)
    return (z ^ 2, x, c) if x != c else (z, 1 - x, 1 - c)


def half_tile_chip(z, x, c):
    return (z ^ 1, x, c)


def place():
    block = lax.axis_index("aux")
    return lax.rem(block // 2, 2) == 0, lax.rem(block, 2), lax.axis_index("pair")


def halves(value):
    high = value.astype(jnp.bfloat16)
    return high, (value - high.astype(jnp.float32)).astype(jnp.bfloat16)


def stack_kernel(order, block, stack):
    pairs, rows = block.shape
    parts = halves(block[...])
    for i, part in enumerate(order):
        stack[pl.ds(i * pairs, pairs), pl.ds(0, rows)] = parts[part]


def scaled_kernel(weight, block, stack):
    pairs, rows = block.shape
    parts = halves(block[...] * weight[...])
    for i, part in enumerate((0, 0, 1)):
        stack[pl.ds(i * pairs, pairs), pl.ds(0, rows)] = parts[part]


def both_kernel(weight, block, stack, scaled):
    stack_kernel((0, 1, 0), block, stack)
    scaled_kernel(weight, block, scaled)


def three_kernel(weight, block, far, stack, scaled, far_stack):
    stack_kernel((0, 1, 0), block, stack)
    stack_kernel((0, 1, 0), far, far_stack)
    scaled_kernel(weight, block, scaled)


def meet_kernel(far, xp, xp_scaled, zn_scaled, mine, theirs):
    even, x, c = place()
    rows = mine.shape[1]
    half = rows // 2
    tiles = lax.dot_general(
        jnp.concatenate([far[...], xp[...]], 1),
        jnp.concatenate([zn_scaled[...], xp_scaled[...]], 1),
        (((0,), (0,)), ((), ())),
        preferred_element_type=jnp.float32,
    )
    far_zn, far_xp = tiles[:rows, :rows], tiles[:rows, 128 : 128 + rows]
    xp_zn = tiles[128 : 128 + rows, :rows]

    def put(core, row, values):
        @pl.when(c == core)
        def _():
            mine[pl.ds(row, values.shape[0]), :] = values

        @pl.when(c != core)
        def _():
            theirs[pl.ds(row, values.shape[0]), :] = values

    put(0, rows, far_zn[:half])
    put(1, rows, far_zn[half:])

    @pl.when(even)
    def _():
        zn_xp = xp_zn.T
        put(0, 0, zn_xp)

        @pl.when(x == 0)
        def _():
            put(1, 0, far_xp)

        @pl.when(x == 1)
        def _():
            put(1, 0, zn_xp)

    @pl.when(~even)
    def _():
        zn_far = far_zn.T
        put(1, 0, zn_far)

        @pl.when(x == 0)
        def _():
            put(0, 0, far_xp)

        @pl.when(x == 1)
        def _():
            put(0, 0, zn_far)


def sum_kernel(mine, theirs, tile, half_tile):
    rows, half = tile.shape[0], half_tile.shape[0]
    tile[...] = mine[pl.ds(0, rows), :] + theirs[pl.ds(0, rows), :]
    half_tile[...] = mine[pl.ds(rows, half), :] + theirs[pl.ds(rows, half), :]


def dot_over_pairs(left, right):
    return lax.dot_general(
        left, right, (((0,), (0,)), ((), ())), preferred_element_type=jnp.float32
    )


def own_kernel(own, own_scaled, own_own):
    rows = own_own.shape[0]
    own_own[...] = dot_over_pairs(own[...], own_scaled[...])[:rows, :rows]


def far_kernel(far, own_scaled, far_own):
    rows = far_own.shape[0]
    far_own[...] = dot_over_pairs(far[...], own_scaled[...])[:rows, :rows]


def local_kernel(own, own_scaled, own_own, far, xp, zn_scaled, mine, theirs):
    _, _, c = place()
    rows = mine.shape[1]
    half = rows // 2
    by_own = dot_over_pairs(jnp.concatenate([far[...], xp[...]], 1), own_scaled[...])
    far_own, xp_own = by_own[:rows, :rows], by_own[128 : 128 + rows, :rows]
    zn_own = dot_over_pairs(zn_scaled[...], own[...])[:rows, :rows]

    def first(kept):
        kept[pl.ds(0, rows), :] = own_own[...]
        kept[pl.ds(rows, rows), :] = xp_own
        kept[pl.ds(2 * rows, half), :] = zn_own[:half]

    def second(kept):
        kept[pl.ds(0, half), :] = zn_own[half:]
        kept[pl.ds(half, rows), :] = jnp.zeros((rows, rows), jnp.float32)
        kept[pl.ds(half + rows, rows), :] = far_own

    @pl.when(c == 0)
    def _():
        first(mine)
        second(theirs)

    @pl.when(c == 1)
    def _():
        first(theirs)
        second(mine)


def local2_kernel(own, own_scaled, own_own, xp, zn_scaled, mine, theirs):
    _, _, c = place()
    rows = mine.shape[1]
    half = rows // 2
    xp_own = dot_over_pairs(xp[...], own_scaled[...])[:rows, :rows]
    zn_own = dot_over_pairs(zn_scaled[...], own[...])[:rows, :rows]

    def first(kept):
        kept[pl.ds(0, rows), :] = own_own[...]
        kept[pl.ds(rows, rows), :] = xp_own
        kept[pl.ds(2 * rows, half), :] = zn_own[:half]

    def second(kept):
        kept[pl.ds(0, half), :] = zn_own[half:]
        kept[pl.ds(half, 2 * rows), :] = jnp.zeros((2 * rows, rows), jnp.float32)

    @pl.when(c == 0)
    def _():
        first(mine)
        second(theirs)

    @pl.when(c == 1)
    def _():
        first(theirs)
        second(mine)


def finish_kernel(mine, theirs, tile, half_tile, response):
    even, x, c = place()
    rows = tile.shape[0]
    half = rows // 2
    response[...] = mine[...] + theirs[...]

    @pl.when((c == 0) & (x == 1))
    def _():
        response[pl.ds(rows, rows), :] = tile[...]

    @pl.when(c == 1)
    def _():
        response[pl.ds(half, rows), :] = tile[...]

    @pl.when((c == 0) & ~even)
    def _():
        response[pl.ds(2 * rows, half), :] = half_tile[...]

    @pl.when((c == 1) & ~even)
    def _():
        response[pl.ds(0, half), :] = half_tile[...]


def finish2_kernel(mine, theirs, far_own, far_own2, tile, half_tile, response):
    even, x, c = place()
    rows = tile.shape[0]
    half = rows // 2
    response[...] = mine[...] + theirs[...]

    @pl.when((c == 0) & (x == 1))
    def _():
        response[pl.ds(rows, rows), :] = tile[...]

    @pl.when(c == 1)
    def _():
        response[pl.ds(half, rows), :] = tile[...]
        response[pl.ds(half + rows, rows), :] = far_own[...] + far_own2[...]

    @pl.when((c == 0) & ~even)
    def _():
        response[pl.ds(2 * rows, half), :] = half_tile[...]

    @pl.when((c == 1) & ~even)
    def _():
        response[pl.ds(0, half), :] = half_tile[...]


def in_vmem(kernel, outs, *operands, flops=1000):
    whole = pl.BlockSpec(memory_space=pltpu.VMEM)
    return pl.pallas_call(
        kernel,
        out_shape=[jax.ShapeDtypeStruct(*out) for out in outs],
        in_specs=[whole] * len(operands),
        out_specs=[whole] * len(outs),
        compiler_params=pltpu.CompilerParams(vmem_limit_bytes=32 * 1024 * 1024),
        cost_estimate=pl.CostEstimate(flops=flops, bytes_accessed=1000, transcendentals=0),
    )(*operands)


def octet_shards(pair_tensor, occ_energy, vir_energy, frequency):
    own = pair_tensor.T
    pairs, rows = own.shape
    weight = jnp.broadcast_to(
        pair_weights(occ_energy, vir_energy, frequency)[:, None], (pairs, rows)
    )
    stack = ((3 * pairs, 128), jnp.bfloat16)
    square, half_square = ((rows, rows), jnp.float32), ((rows // 2, rows), jnp.float32)
    plain = functools.partial(stack_kernel, (0, 1, 0))
    far = sent(own, far_chip)
    xp = sent(own, other_x)
    zn = sent(own, next_chip)
    xp_stack, xp_scaled, far_stack = in_vmem(three_kernel, [stack] * 3, weight, xp, far)
    zn, xp_scaled = lax.optimization_barrier((zn, xp_scaled))
    (zn_scaled,) = in_vmem(scaled_kernel, [stack], weight, zn)
    (own_stack,) = in_vmem(plain, [stack], own)
    (own_scaled,) = in_vmem(scaled_kernel, [stack], weight, own)
    (own_own,) = in_vmem(own_kernel, [square], own_stack, own_scaled)
    parts = ((3 * rows // 2, rows), jnp.float32)
    mine, theirs = in_vmem(
        meet_kernel, [parts] * 2, far_stack, xp_stack, xp_scaled, zn_scaled, flops=1000
    )
    tile, half_tile = in_vmem(
        sum_kernel, [square, half_square], mine, sent(theirs, other_core)
    )
    tile = sent(tile, tile_chip)
    half_tile = sent(half_tile, half_tile_chip)
    kept = ((5 * rows // 2, rows), jnp.float32)
    mine, theirs = in_vmem(
        local_kernel, [kept] * 2, own_stack, own_scaled, own_own, far_stack, xp_stack, zn_scaled, flops=1000
    )
    (response,) = in_vmem(
        finish_kernel, [kept], mine, sent(theirs, other_core), tile, half_tile
    )
    return response.T


def solution(mesh):
    in_specs = (P(("parts", "aux"), "pair"), P(("parts", "pair")), P("parts"), P("parts"))
    out_specs = P(("parts", "aux"), "pair")
    octet = mesh.shape["aux"] == 8 and mesh.shape["pair"] == 2
    shards = octet_shards if octet else ring_shards
    return jax.shard_map(shards, mesh=mesh, in_specs=in_specs, out_specs=out_specs, check_vma=False)
```

```python
import functools

import jax
import jax.numpy as jnp
from jax import lax
from jax.experimental import pallas as pl
from jax.experimental.pallas import tpu as pltpu
from jax.sharding import PartitionSpec as P


def passed_along(value, axis, by):
    peers = lax.axis_size(axis)
    return lax.ppermute(value, axis, [(i, (i + by) % peers) for i in range(peers)])


def pair_weights(occ_energy, vir_energy, frequency):
    energy_gap = vir_energy[None, :] - occ_energy[:, None]
    return (4.0 * energy_gap / (energy_gap * energy_gap + frequency[0] * frequency[0])).reshape(-1)


def product_tile(scaled_rows, block_rows):
    return lax.dot_general(
        scaled_rows,
        block_rows,
        (((1,), (1,)), ((), ())),
        precision=lax.Precision.HIGHEST,
        preferred_element_type=jnp.float32,
    )


def write_block(collected, values, column):
    return lax.dynamic_update_slice_in_dim(collected, values, column, 1)


def half_turn(scaled_rows, first_block, half_span):
    row_count = scaled_rows.shape[0]
    collected = jnp.zeros((row_count, (half_span + 1) * row_count), jnp.float32)
    collected = write_block(collected, product_tile(scaled_rows, first_block), 0)
    opposite = passed_along(first_block, "aux", -half_span)
    collected = write_block(collected, product_tile(scaled_rows, opposite), half_span * row_count)

    def advance(turn_index, loop_state):
        collected, forward, backward = loop_state
        forward = passed_along(forward, "aux", -1)
        backward = passed_along(backward, "aux", 1)
        collected = write_block(
            collected, product_tile(scaled_rows, forward), turn_index * row_count
        )
        collected = write_block(
            collected, product_tile(scaled_rows, backward), (half_span - turn_index) * row_count
        )
        return (collected, forward, backward)

    collected, forward, backward = lax.fori_loop(
        1, half_span // 2, advance, (collected, first_block, opposite)
    )
    middle = passed_along(forward, "aux", -1)
    return write_block(collected, product_tile(scaled_rows, middle), half_span // 2 * row_count)


def ring_shards(pair_tensor, occ_energy, vir_energy, frequency):
    n_aux = lax.axis_size("aux")
    scaled_rows = pair_tensor * pair_weights(occ_energy, vir_energy, frequency)[None, :]
    collected = half_turn(scaled_rows, pair_tensor, n_aux // 2)
    return lax.psum_scatter(collected, "pair", scatter_dimension=1, tiled=True)


def sent(value, target_of):
    pairs = []
    for z in range(4):
        for x in range(2):
            for c in range(2):
                tz, tx, tc = target_of(z, x, c)
                pairs.append(((z * 2 + x) * 2 + c, (tz * 2 + tx) * 2 + tc))
    return lax.ppermute(value, ("aux", "pair"), pairs)


def other_core(z, x, c):
    return (z, x, 1 - c)


ORDERS = (("xp", "zn", "far"), ("far", "zn", "xp"))


def far_chip(z, x, c):
    return (z ^ 2, x, c)


def other_x(z, x, c):
    return (z, 1 - x, c)


def next_chip(z, x, c):
    return (z ^ 1, x if z % 2 else 1 - x, c)


def tile_chip(z, x, c):
    if z % 2 == 0:
        return (z, 1 - x, c)
    return (z ^ 2, x, c) if x != c else (z, 1 - x, 1 - c)


def half_tile_chip(z, x, c):
    return (z ^ 1, x, c)


def place():
    block = lax.axis_index("aux")
    return lax.rem(block // 2, 2) == 0, lax.rem(block, 2), lax.axis_index("pair")


def halves(value):
    high = value.astype(jnp.bfloat16)
    return high, (value - high.astype(jnp.float32)).astype(jnp.bfloat16)


def product(left, right):
    return (
        jnp.dot(left[0], right[0], preferred_element_type=jnp.float32)
        + jnp.dot(left[1], right[0], preferred_element_type=jnp.float32)
        + jnp.dot(left[0], right[1], preferred_element_type=jnp.float32)
    )


def left_kernel(block, left):
    left[0], left[1] = halves(block[...].T)


def right_kernel(weight, block, right):
    columns = pl.ds(0, block.shape[1])
    right[0, :, columns], right[1, :, columns] = halves(block[...] * weight[...])


def ready_kernel(orders, weight, *refs):
    blocks, (far_left, xp_left, xp_right, zn_right) = refs[:3], refs[3:]
    _, _, c = place()
    for core, order in enumerate(orders):

        @pl.when(c == core)
        def _():
            left_kernel(blocks[order.index("far")], far_left)
            left_kernel(blocks[order.index("xp")], xp_left)
            right_kernel(weight, blocks[order.index("xp")], xp_right)
            right_kernel(weight, blocks[order.index("zn")], zn_right)


def meet_kernel(far, xp, xp_scaled, zn_scaled, mine, theirs):
    even, x, c = place()
    rows = mine.shape[1]
    half = rows // 2
    scaled = [jnp.concatenate([zn_scaled[i], xp_scaled[i]], 1) for i in range(2)]
    by_far = product(far, scaled)
    far_zn, far_xp = by_far[:, :rows], by_far[:, 128 : 128 + rows]
    xp_zn = product(xp, zn_scaled)[:, :rows]

    def put(core, row, values):
        @pl.when(c == core)
        def _():
            mine[pl.ds(row, values.shape[0]), :] = values

        @pl.when(c != core)
        def _():
            theirs[pl.ds(row, values.shape[0]), :] = values

    put(0, rows, far_zn[:half])
    put(1, rows, far_zn[half:])

    @pl.when(even)
    def _():
        zn_xp = xp_zn.T
        put(0, 0, zn_xp)

        @pl.when(x == 0)
        def _():
            put(1, 0, far_xp)

        @pl.when(x == 1)
        def _():
            put(1, 0, zn_xp)

    @pl.when(~even)
    def _():
        zn_far = far_zn.T
        put(1, 0, zn_far)

        @pl.when(x == 0)
        def _():
            put(0, 0, far_xp)

        @pl.when(x == 1)
        def _():
            put(0, 0, zn_far)


def sum_kernel(mine, theirs, tile, half_tile):
    rows, half = tile.shape[0], half_tile.shape[0]
    tile[...] = mine[pl.ds(0, rows), :] + theirs[pl.ds(0, rows), :]
    half_tile[...] = mine[pl.ds(rows, half), :] + theirs[pl.ds(rows, half), :]


def own_kernel(own, own_scaled, own_own):
    own_own[...] = product(own, own_scaled)[:, : own_own.shape[1]]


def local_kernel(own, own_scaled, own_own, far, xp, zn_scaled, mine, theirs):
    _, _, c = place()
    rows = mine.shape[1]
    half = rows // 2
    far_own = product(far, own_scaled)[:, :rows]
    xp_own = product(xp, own_scaled)[:, :rows]
    zn_own = product(own, zn_scaled)[:, :rows].T

    def first(kept):
        kept[pl.ds(0, rows), :] = own_own[...]
        kept[pl.ds(rows, rows), :] = xp_own
        kept[pl.ds(2 * rows, half), :] = zn_own[:half]

    def second(kept):
        kept[pl.ds(0, half), :] = zn_own[half:]
        kept[pl.ds(half, rows), :] = jnp.zeros((rows, rows), jnp.float32)
        kept[pl.ds(half + rows, rows), :] = far_own

    @pl.when(c == 0)
    def _():
        first(mine)
        second(theirs)

    @pl.when(c == 1)
    def _():
        first(theirs)
        second(mine)


def finish_kernel(mine, theirs, tile, half_tile, response):
    even, x, c = place()
    rows = tile.shape[0]
    half = rows // 2
    response[...] = mine[...] + theirs[...]

    @pl.when((c == 0) & (x == 1))
    def _():
        response[pl.ds(rows, rows), :] = tile[...]

    @pl.when(c == 1)
    def _():
        response[pl.ds(half, rows), :] = tile[...]

    @pl.when((c == 0) & ~even)
    def _():
        response[pl.ds(2 * rows, half), :] = half_tile[...]

    @pl.when((c == 1) & ~even)
    def _():
        response[pl.ds(0, half), :] = half_tile[...]


def in_vmem(kernel, outs, *operands, flops=1000):
    whole = pl.BlockSpec(memory_space=pltpu.VMEM)
    return pl.pallas_call(
        kernel,
        out_shape=[jax.ShapeDtypeStruct(*out) for out in outs],
        in_specs=[whole] * len(operands),
        out_specs=[whole] * len(outs),
        compiler_params=pltpu.CompilerParams(vmem_limit_bytes=32 * 1024 * 1024),
        cost_estimate=pl.CostEstimate(flops=flops, bytes_accessed=1000, transcendentals=0),
    )(*operands)


def octet_shards(pair_tensor, occ_energy, vir_energy, frequency):
    own = pair_tensor.T
    pairs, rows = own.shape
    weight = jnp.broadcast_to(
        pair_weights(occ_energy, vir_energy, frequency)[:, None], (pairs, rows)
    )
    left, right = ((2, rows, pairs), jnp.bfloat16), ((2, pairs, 128), jnp.bfloat16)
    square, half_square = ((rows, rows), jnp.float32), ((rows // 2, rows), jnp.float32)
    routes = {"far": far_chip, "xp": other_x, "zn": next_chip}
    blocks = [
        sent(own, lambda z, x, c, slot=slot: routes[ORDERS[c][slot]](z, x, c)) for slot in range(3)
    ]
    far_left, xp_left, xp_right, zn_right = in_vmem(
        functools.partial(ready_kernel, ORDERS), [left, left, right, right], weight, *blocks
    )
    (own_left,) = in_vmem(left_kernel, [left], own)
    (own_right,) = in_vmem(right_kernel, [right], weight, own)
    (own_own,) = in_vmem(own_kernel, [square], own_left, own_right)
    parts = ((3 * rows // 2, rows), jnp.float32)
    mine, theirs = in_vmem(meet_kernel, [parts] * 2, far_left, xp_left, xp_right, zn_right)
    tile, half_tile = in_vmem(
        sum_kernel, [square, half_square], mine, sent(theirs, other_core)
    )
    tile = sent(tile, tile_chip)
    half_tile = sent(half_tile, half_tile_chip)
    kept = ((5 * rows // 2, rows), jnp.float32)
    mine, theirs = in_vmem(
        local_kernel, [kept] * 2, own_left, own_right, own_own, far_left, xp_left, zn_right
    )
    (response,) = in_vmem(
        finish_kernel, [kept], mine, sent(theirs, other_core), tile, half_tile
    )
    return response.T


def solution(mesh):
    in_specs = (P(("parts", "aux"), "pair"), P(("parts", "pair")), P("parts"), P("parts"))
    out_specs = P(("parts", "aux"), "pair")
    octet = mesh.shape["aux"] == 8 and mesh.shape["pair"] == 2
    shards = octet_shards if octet else ring_shards
    return jax.shard_map(shards, mesh=mesh, in_specs=in_specs, out_specs=out_specs, check_vma=False)
```

```python
import functools

import jax
import jax.numpy as jnp
from jax import lax
from jax.experimental import pallas as pl
from jax.experimental.pallas import tpu as pltpu
from jax.sharding import PartitionSpec as P


def passed_along(value, axis, by):
    peers = lax.axis_size(axis)
    return lax.ppermute(value, axis, [(i, (i + by) % peers) for i in range(peers)])


def pair_weights(occ_energy, vir_energy, frequency):
    energy_gap = vir_energy[None, :] - occ_energy[:, None]
    return (4.0 * energy_gap / (energy_gap * energy_gap + frequency[0] * frequency[0])).reshape(-1)


def product_tile(scaled_rows, block_rows):
    return lax.dot_general(
        scaled_rows,
        block_rows,
        (((1,), (1,)), ((), ())),
        precision=lax.Precision.HIGHEST,
        preferred_element_type=jnp.float32,
    )


def write_block(collected, values, column):
    return lax.dynamic_update_slice_in_dim(collected, values, column, 1)


def half_turn(scaled_rows, first_block, half_span):
    row_count = scaled_rows.shape[0]
    collected = jnp.zeros((row_count, (half_span + 1) * row_count), jnp.float32)
    collected = write_block(collected, product_tile(scaled_rows, first_block), 0)
    opposite = passed_along(first_block, "aux", -half_span)
    collected = write_block(collected, product_tile(scaled_rows, opposite), half_span * row_count)

    def advance(turn_index, loop_state):
        collected, forward, backward = loop_state
        forward = passed_along(forward, "aux", -1)
        backward = passed_along(backward, "aux", 1)
        collected = write_block(
            collected, product_tile(scaled_rows, forward), turn_index * row_count
        )
        collected = write_block(
            collected, product_tile(scaled_rows, backward), (half_span - turn_index) * row_count
        )
        return (collected, forward, backward)

    collected, forward, backward = lax.fori_loop(
        1, half_span // 2, advance, (collected, first_block, opposite)
    )
    middle = passed_along(forward, "aux", -1)
    return write_block(collected, product_tile(scaled_rows, middle), half_span // 2 * row_count)


def ring_shards(pair_tensor, occ_energy, vir_energy, frequency):
    n_aux = lax.axis_size("aux")
    scaled_rows = pair_tensor * pair_weights(occ_energy, vir_energy, frequency)[None, :]
    collected = half_turn(scaled_rows, pair_tensor, n_aux // 2)
    return lax.psum_scatter(collected, "pair", scatter_dimension=1, tiled=True)


def sent(value, target_of):
    pairs = []
    for z in range(4):
        for x in range(2):
            for c in range(2):
                tz, tx, tc = target_of(z, x, c)
                pairs.append(((z * 2 + x) * 2 + c, (tz * 2 + tx) * 2 + tc))
    return lax.ppermute(value, ("aux", "pair"), pairs)


def other_core(z, x, c):
    return (z, x, 1 - c)


ORDERS = (("xp", "zn", "far"), ("far", "zn", "xp"))


def far_chip(z, x, c):
    return (z ^ 2, x, c)


def other_x(z, x, c):
    return (z, 1 - x, c)


def next_chip(z, x, c):
    return (z ^ 1, x if z % 2 else 1 - x, c)


def tile_chip(z, x, c):
    return (z ^ 2, x, c) if z % 2 and x != c else (z, 1 - x, 1 - c)


def half_tile_chip(z, x, c):
    return (z ^ 1, x, c)


def place():
    block = lax.axis_index("aux")
    return lax.rem(block // 2, 2) == 0, lax.rem(block, 2), lax.axis_index("pair")


def halves(value):
    high = value.astype(jnp.bfloat16)
    return high, (value - high.astype(jnp.float32)).astype(jnp.bfloat16)


def product(left, right):
    return (
        jnp.dot(left[0], right[0], preferred_element_type=jnp.float32)
        + jnp.dot(left[1], right[0], preferred_element_type=jnp.float32)
        + jnp.dot(left[0], right[1], preferred_element_type=jnp.float32)
    )


def left_kernel(block, left):
    left[0], left[1] = halves(block[...].T)


def right_kernel(weight, block, right):
    columns = pl.ds(0, block.shape[1])
    right[0, :, columns], right[1, :, columns] = halves(block[...] * weight[...])


def ready_kernel(orders, weight, *refs):
    blocks, (far_left, xp_left, xp_right, zn_right) = refs[:3], refs[3:]
    _, _, c = place()
    for core, order in enumerate(orders):

        @pl.when(c == core)
        def _():
            left_kernel(blocks[order.index("far")], far_left)
            left_kernel(blocks[order.index("xp")], xp_left)
            right_kernel(weight, blocks[order.index("xp")], xp_right)
            right_kernel(weight, blocks[order.index("zn")], zn_right)


def meet_kernel(far, xp, xp_scaled, zn_scaled, mine, theirs):
    even, x, c = place()
    rows = mine.shape[1]
    half = rows // 2
    scaled = [jnp.concatenate([zn_scaled[i], xp_scaled[i]], 1) for i in range(2)]
    by_far = product(far, scaled)
    far_zn, far_xp = by_far[:, :rows], by_far[:, 128 : 128 + rows]
    xp_zn = product(xp, zn_scaled)[:, :rows]

    def put(core, row, values):
        @pl.when(c == core)
        def _():
            mine[pl.ds(row, values.shape[0]), :] = values

        @pl.when(c != core)
        def _():
            theirs[pl.ds(row, values.shape[0]), :] = values

    put(0, rows, far_zn[:half])
    put(1, rows, far_zn[half:])

    @pl.when(even)
    def _():
        zn_xp = xp_zn.T
        put(1, 0, zn_xp)

        @pl.when(x == 0)
        def _():
            put(0, 0, far_xp)

        @pl.when(x == 1)
        def _():
            put(0, 0, zn_xp)

    @pl.when(~even)
    def _():
        zn_far = far_zn.T
        put(1, 0, zn_far)

        @pl.when(x == 0)
        def _():
            put(0, 0, far_xp)

        @pl.when(x == 1)
        def _():
            put(0, 0, zn_far)


def sum_kernel(mine, theirs, tile, half_tile):
    rows, half = tile.shape[0], half_tile.shape[0]
    tile[...] = mine[pl.ds(0, rows), :] + theirs[pl.ds(0, rows), :]
    half_tile[...] = mine[pl.ds(rows, half), :] + theirs[pl.ds(rows, half), :]


def own_kernel(own, own_scaled, own_own):
    own_own[...] = product(own, own_scaled)[:, : own_own.shape[1]]


def local_kernel(own, own_scaled, own_own, far, xp, zn_scaled, mine, theirs):
    _, _, c = place()
    rows = mine.shape[1]
    half = rows // 2
    far_own = product(far, own_scaled)[:, :rows]
    xp_own = product(xp, own_scaled)[:, :rows]
    zn_own = product(own, zn_scaled)[:, :rows].T

    def first(kept):
        kept[pl.ds(0, rows), :] = own_own[...]
        kept[pl.ds(rows, rows), :] = xp_own
        kept[pl.ds(2 * rows, half), :] = zn_own[:half]

    def second(kept):
        kept[pl.ds(0, half), :] = zn_own[half:]
        kept[pl.ds(half, rows), :] = jnp.zeros((rows, rows), jnp.float32)
        kept[pl.ds(half + rows, rows), :] = far_own

    @pl.when(c == 0)
    def _():
        first(mine)
        second(theirs)

    @pl.when(c == 1)
    def _():
        first(theirs)
        second(mine)


def finish_kernel(mine, theirs, tile, half_tile, response):
    even, x, c = place()
    rows = tile.shape[0]
    half = rows // 2
    response[...] = mine[...] + theirs[...]

    @pl.when((c == 0) & (x == 1))
    def _():
        response[pl.ds(rows, rows), :] = tile[...]

    @pl.when(c == 1)
    def _():
        response[pl.ds(half, rows), :] = tile[...]

    @pl.when((c == 0) & ~even)
    def _():
        response[pl.ds(2 * rows, half), :] = half_tile[...]

    @pl.when((c == 1) & ~even)
    def _():
        response[pl.ds(0, half), :] = half_tile[...]


def in_vmem(kernel, outs, *operands, flops=1000):
    whole = pl.BlockSpec(memory_space=pltpu.VMEM)
    return pl.pallas_call(
        kernel,
        out_shape=[jax.ShapeDtypeStruct(*out) for out in outs],
        in_specs=[whole] * len(operands),
        out_specs=[whole] * len(outs),
        compiler_params=pltpu.CompilerParams(vmem_limit_bytes=32 * 1024 * 1024),
        cost_estimate=pl.CostEstimate(flops=flops, bytes_accessed=1000, transcendentals=0),
    )(*operands)


def octet_shards(pair_tensor, occ_energy, vir_energy, frequency):
    own = pair_tensor.T
    pairs, rows = own.shape
    weight = jnp.broadcast_to(
        pair_weights(occ_energy, vir_energy, frequency)[:, None], (pairs, rows)
    )
    left, right = ((2, rows, pairs), jnp.bfloat16), ((2, pairs, 128), jnp.bfloat16)
    square, half_square = ((rows, rows), jnp.float32), ((rows // 2, rows), jnp.float32)
    routes = {"far": far_chip, "xp": other_x, "zn": next_chip}
    blocks = [
        sent(own, lambda z, x, c, slot=slot: routes[ORDERS[c][slot]](z, x, c)) for slot in range(3)
    ]
    far_left, xp_left, xp_right, zn_right = in_vmem(
        functools.partial(ready_kernel, ORDERS), [left, left, right, right], weight, *blocks
    )
    (own_left,) = in_vmem(left_kernel, [left], own)
    (own_right,) = in_vmem(right_kernel, [right], weight, own)
    (own_own,) = in_vmem(own_kernel, [square], own_left, own_right)
    parts = ((3 * rows // 2, rows), jnp.float32)
    mine, theirs = in_vmem(meet_kernel, [parts] * 2, far_left, xp_left, xp_right, zn_right)
    tile, half_tile = in_vmem(
        sum_kernel, [square, half_square], mine, sent(theirs, other_core)
    )
    tile = sent(tile, tile_chip)
    half_tile = sent(half_tile, half_tile_chip)
    kept = ((5 * rows // 2, rows), jnp.float32)
    mine, theirs = in_vmem(
        local_kernel, [kept] * 2, own_left, own_right, own_own, far_left, xp_left, zn_right
    )
    (response,) = in_vmem(
        finish_kernel, [kept], mine, sent(theirs, other_core), tile, half_tile
    )
    return response.T


def solution(mesh):
    in_specs = (P(("parts", "aux"), "pair"), P(("parts", "pair")), P("parts"), P("parts"))
    out_specs = P(("parts", "aux"), "pair")
    octet = mesh.shape["aux"] == 8 and mesh.shape["pair"] == 2
    shards = octet_shards if octet else ring_shards
    return jax.shard_map(shards, mesh=mesh, in_specs=in_specs, out_specs=out_specs, check_vma=False)
```

```python
import functools

import jax
import jax.numpy as jnp
from jax import lax
from jax.experimental import pallas as pl
from jax.experimental.pallas import tpu as pltpu
from jax.sharding import PartitionSpec as P


def passed_along(value, axis, by):
    peers = lax.axis_size(axis)
    return lax.ppermute(value, axis, [(i, (i + by) % peers) for i in range(peers)])


def pair_weights(occ_energy, vir_energy, frequency):
    energy_gap = vir_energy[None, :] - occ_energy[:, None]
    return (4.0 * energy_gap / (energy_gap * energy_gap + frequency[0] * frequency[0])).reshape(-1)


def product_tile(scaled_rows, block_rows):
    return lax.dot_general(
        scaled_rows,
        block_rows,
        (((1,), (1,)), ((), ())),
        precision=lax.Precision.HIGHEST,
        preferred_element_type=jnp.float32,
    )


def write_block(collected, values, column):
    return lax.dynamic_update_slice_in_dim(collected, values, column, 1)


def half_turn(scaled_rows, first_block, half_span):
    row_count = scaled_rows.shape[0]
    collected = jnp.zeros((row_count, (half_span + 1) * row_count), jnp.float32)
    collected = write_block(collected, product_tile(scaled_rows, first_block), 0)
    opposite = passed_along(first_block, "aux", -half_span)
    collected = write_block(collected, product_tile(scaled_rows, opposite), half_span * row_count)

    def advance(turn_index, loop_state):
        collected, forward, backward = loop_state
        forward = passed_along(forward, "aux", -1)
        backward = passed_along(backward, "aux", 1)
        collected = write_block(
            collected, product_tile(scaled_rows, forward), turn_index * row_count
        )
        collected = write_block(
            collected, product_tile(scaled_rows, backward), (half_span - turn_index) * row_count
        )
        return (collected, forward, backward)

    collected, forward, backward = lax.fori_loop(
        1, half_span // 2, advance, (collected, first_block, opposite)
    )
    middle = passed_along(forward, "aux", -1)
    return write_block(collected, product_tile(scaled_rows, middle), half_span // 2 * row_count)


def ring_shards(pair_tensor, occ_energy, vir_energy, frequency):
    n_aux = lax.axis_size("aux")
    scaled_rows = pair_tensor * pair_weights(occ_energy, vir_energy, frequency)[None, :]
    collected = half_turn(scaled_rows, pair_tensor, n_aux // 2)
    return lax.psum_scatter(collected, "pair", scatter_dimension=1, tiled=True)


def sent(value, target_of):
    pairs = []
    for z in range(4):
        for x in range(2):
            for c in range(2):
                tz, tx, tc = target_of(z, x, c)
                pairs.append(((z * 2 + x) * 2 + c, (tz * 2 + tx) * 2 + tc))
    return lax.ppermute(value, ("aux", "pair"), pairs)


def other_core(z, x, c):
    return (z, x, 1 - c)


ORDERS = (("xp", "zn", "far"), ("far", "zn", "xp"))


def far_chip(z, x, c):
    return (z ^ 2, x, c)


def other_x(z, x, c):
    return (z, 1 - x, c)


def next_chip(z, x, c):
    return (z ^ 1, x if z % 2 else 1 - x, c)


def tile_chip(z, x, c):
    return (z ^ 2, x, c) if z % 2 and x != c else (z, 1 - x, 1 - c)


def half_tile_chip(z, x, c):
    return (z ^ 1, x, c)


def place():
    block = lax.axis_index("aux")
    return lax.rem(block // 2, 2) == 0, lax.rem(block, 2), lax.axis_index("pair")


def halves(value):
    high = value.astype(jnp.bfloat16)
    return high, (value - high.astype(jnp.float32)).astype(jnp.bfloat16)


def product(left, right):
    return (
        jnp.dot(left[0], right[0], preferred_element_type=jnp.float32)
        + jnp.dot(left[1], right[0], preferred_element_type=jnp.float32)
        + jnp.dot(left[0], right[1], preferred_element_type=jnp.float32)
    )


def left_kernel(block, left):
    left[0], left[1] = halves(block[...].T)


def right_kernel(weight, block, right):
    columns = pl.ds(0, block.shape[1])
    right[0, :, columns], right[1, :, columns] = halves(block[...] * weight[...])


def ready_kernel(orders, weight, *refs):
    blocks, (far_left, xp_left, xp_right, zn_right) = refs[:3], refs[3:]
    even, x, c = place()
    for core, order in enumerate(orders):

        @pl.when(c == core)
        def _():
            left_kernel(blocks[order.index("far")], far_left)
            right_kernel(weight, blocks[order.index("zn")], zn_right)

            @pl.when(even | (x == 0))
            def _():
                left_kernel(blocks[order.index("xp")], xp_left)
                right_kernel(weight, blocks[order.index("xp")], xp_right)

            @pl.when(~even & (x == 1))
            def _():
                xp_left[...] = jnp.zeros_like(xp_left)
                xp_right[...] = jnp.zeros_like(xp_right)


def meet_kernel(far, xp, xp_scaled, zn_scaled, mine, theirs):
    even, x, c = place()
    rows = mine.shape[1]
    half = rows // 2
    scaled = [jnp.concatenate([zn_scaled[i], xp_scaled[i]], 1) for i in range(2)]
    by_far = product(far, scaled)
    far_zn, far_xp = by_far[:, :rows], by_far[:, 128 : 128 + rows]

    def put(core, row, values):
        @pl.when(c == core)
        def _():
            mine[pl.ds(row, values.shape[0]), :] = values

        @pl.when(c != core)
        def _():
            theirs[pl.ds(row, values.shape[0]), :] = values

    put(0, rows, far_zn[:half])
    put(1, rows, far_zn[half:])

    @pl.when(even)
    def _():
        zn_xp = product(xp, zn_scaled)[:, :rows].T
        put(1, 0, zn_xp)

        @pl.when(x == 0)
        def _():
            put(0, 0, far_xp)

        @pl.when(x == 1)
        def _():
            put(0, 0, zn_xp)

    @pl.when(~even)
    def _():
        zn_far = far_zn.T
        put(1, 0, zn_far)

        @pl.when(x == 0)
        def _():
            put(0, 0, far_xp)

        @pl.when(x == 1)
        def _():
            put(0, 0, zn_far)


def sum_kernel(mine, theirs, tile, half_tile):
    rows, half = tile.shape[0], half_tile.shape[0]
    tile[...] = mine[pl.ds(0, rows), :] + theirs[pl.ds(0, rows), :]
    half_tile[...] = mine[pl.ds(rows, half), :] + theirs[pl.ds(rows, half), :]


def own_kernel(own, own_scaled, own_own):
    own_own[...] = product(own, own_scaled)[:, : own_own.shape[1]]


def local_kernel(own, own_scaled, own_own, far, xp, zn_scaled, mine, theirs):
    _, _, c = place()
    rows = mine.shape[1]
    half = rows // 2
    far_own = product(far, own_scaled)[:, :rows]
    xp_own = product(xp, own_scaled)[:, :rows]
    zn_own = product(own, zn_scaled)[:, :rows].T

    def first(kept):
        kept[pl.ds(0, rows), :] = own_own[...]
        kept[pl.ds(rows, rows), :] = xp_own
        kept[pl.ds(2 * rows, half), :] = zn_own[:half]

    def second(kept):
        kept[pl.ds(0, half), :] = zn_own[half:]
        kept[pl.ds(half, rows), :] = jnp.zeros((rows, rows), jnp.float32)
        kept[pl.ds(half + rows, rows), :] = far_own

    @pl.when(c == 0)
    def _():
        first(mine)
        second(theirs)

    @pl.when(c == 1)
    def _():
        first(theirs)
        second(mine)


def finish_kernel(mine, theirs, tile, half_tile, response):
    even, x, c = place()
    rows = tile.shape[0]
    half = rows // 2
    response[...] = mine[...] + theirs[...]

    @pl.when((c == 0) & (x == 1))
    def _():
        response[pl.ds(rows, rows), :] = tile[...]

    @pl.when(c == 1)
    def _():
        response[pl.ds(half, rows), :] = tile[...]

    @pl.when((c == 0) & ~even)
    def _():
        response[pl.ds(2 * rows, half), :] = half_tile[...]

    @pl.when((c == 1) & ~even)
    def _():
        response[pl.ds(0, half), :] = half_tile[...]


def in_vmem(kernel, outs, *operands, flops=1000):
    whole = pl.BlockSpec(memory_space=pltpu.VMEM)
    return pl.pallas_call(
        kernel,
        out_shape=[jax.ShapeDtypeStruct(*out) for out in outs],
        in_specs=[whole] * len(operands),
        out_specs=[whole] * len(outs),
        compiler_params=pltpu.CompilerParams(vmem_limit_bytes=32 * 1024 * 1024),
        cost_estimate=pl.CostEstimate(flops=flops, bytes_accessed=1000, transcendentals=0),
    )(*operands)


def octet_shards(pair_tensor, occ_energy, vir_energy, frequency):
    own = pair_tensor.T
    pairs, rows = own.shape
    weight = jnp.broadcast_to(
        pair_weights(occ_energy, vir_energy, frequency)[:, None], (pairs, rows)
    )
    left, right = ((2, rows, pairs), jnp.bfloat16), ((2, pairs, 128), jnp.bfloat16)
    square, half_square = ((rows, rows), jnp.float32), ((rows // 2, rows), jnp.float32)
    routes = {"far": far_chip, "xp": other_x, "zn": next_chip}
    blocks = [
        sent(own, lambda z, x, c, slot=slot: routes[ORDERS[c][slot]](z, x, c)) for slot in range(3)
    ]
    far_left, xp_left, xp_right, zn_right = in_vmem(
        functools.partial(ready_kernel, ORDERS), [left, left, right, right], weight, *blocks
    )
    (own_left,) = in_vmem(left_kernel, [left], own)
    (own_right,) = in_vmem(right_kernel, [right], weight, own)
    (own_own,) = in_vmem(own_kernel, [square], own_left, own_right)
    parts = ((3 * rows // 2, rows), jnp.float32)
    mine, theirs = in_vmem(meet_kernel, [parts] * 2, far_left, xp_left, xp_right, zn_right)
    tile, half_tile = in_vmem(
        sum_kernel, [square, half_square], mine, sent(theirs, other_core)
    )
    tile = sent(tile, tile_chip)
    half_tile = sent(half_tile, half_tile_chip)
    kept = ((5 * rows // 2, rows), jnp.float32)
    mine, theirs = in_vmem(
        local_kernel, [kept] * 2, own_left, own_right, own_own, far_left, xp_left, zn_right
    )
    (response,) = in_vmem(
        finish_kernel, [kept], mine, sent(theirs, other_core), tile, half_tile
    )
    return response.T


def solution(mesh):
    in_specs = (P(("parts", "aux"), "pair"), P(("parts", "pair")), P("parts"), P("parts"))
    out_specs = P(("parts", "aux"), "pair")
    octet = mesh.shape["aux"] == 8 and mesh.shape["pair"] == 2
    shards = octet_shards if octet else ring_shards
    return jax.shard_map(shards, mesh=mesh, in_specs=in_specs, out_specs=out_specs, check_vma=False)
```

```python
import functools

import jax
import jax.numpy as jnp
from jax import lax
from jax.experimental import pallas as pl
from jax.experimental.pallas import tpu as pltpu
from jax.sharding import PartitionSpec as P


def passed_along(value, axis, by):
    peers = lax.axis_size(axis)
    return lax.ppermute(value, axis, [(i, (i + by) % peers) for i in range(peers)])


def pair_weights(occ_energy, vir_energy, frequency):
    energy_gap = vir_energy[None, :] - occ_energy[:, None]
    return (4.0 * energy_gap / (energy_gap * energy_gap + frequency[0] * frequency[0])).reshape(-1)


def product_tile(scaled_rows, block_rows):
    return lax.dot_general(
        scaled_rows,
        block_rows,
        (((1,), (1,)), ((), ())),
        precision=lax.Precision.HIGHEST,
        preferred_element_type=jnp.float32,
    )


def write_block(collected, values, column):
    return lax.dynamic_update_slice_in_dim(collected, values, column, 1)


def half_turn(scaled_rows, first_block, half_span):
    row_count = scaled_rows.shape[0]
    collected = jnp.zeros((row_count, (half_span + 1) * row_count), jnp.float32)
    collected = write_block(collected, product_tile(scaled_rows, first_block), 0)
    opposite = passed_along(first_block, "aux", -half_span)
    collected = write_block(collected, product_tile(scaled_rows, opposite), half_span * row_count)

    def advance(turn_index, loop_state):
        collected, forward, backward = loop_state
        forward = passed_along(forward, "aux", -1)
        backward = passed_along(backward, "aux", 1)
        collected = write_block(
            collected, product_tile(scaled_rows, forward), turn_index * row_count
        )
        collected = write_block(
            collected, product_tile(scaled_rows, backward), (half_span - turn_index) * row_count
        )
        return (collected, forward, backward)

    collected, forward, backward = lax.fori_loop(
        1, half_span // 2, advance, (collected, first_block, opposite)
    )
    middle = passed_along(forward, "aux", -1)
    return write_block(collected, product_tile(scaled_rows, middle), half_span // 2 * row_count)


def ring_shards(pair_tensor, occ_energy, vir_energy, frequency):
    n_aux = lax.axis_size("aux")
    scaled_rows = pair_tensor * pair_weights(occ_energy, vir_energy, frequency)[None, :]
    collected = half_turn(scaled_rows, pair_tensor, n_aux // 2)
    return lax.psum_scatter(collected, "pair", scatter_dimension=1, tiled=True)


def sent(value, target_of):
    pairs = []
    for z in range(4):
        for x in range(2):
            for c in range(2):
                tz, tx, tc = target_of(z, x, c)
                pairs.append(((z * 2 + x) * 2 + c, (tz * 2 + tx) * 2 + tc))
    return lax.ppermute(value, ("aux", "pair"), pairs)


def other_core(z, x, c):
    return (z, x, 1 - c)


ORDERS = (("zn", "xp", "far"), ("far", "zn", "xp"))


def far_chip(z, x, c):
    return (z ^ 2, x, c)


def other_x(z, x, c):
    return (z, 1 - x, c)


def next_chip(z, x, c):
    return (z ^ 1, x if z % 2 else 1 - x, c)


def tile_chip(z, x, c):
    return (z ^ 2, x, c) if z % 2 and x != c else (z, 1 - x, 1 - c)


def half_tile_chip(z, x, c):
    return (z ^ 1, x, c)


def place():
    block = lax.axis_index("aux")
    return lax.rem(block // 2, 2) == 0, lax.rem(block, 2), lax.axis_index("pair")


def halves(value):
    high = value.astype(jnp.bfloat16)
    return high, (value - high.astype(jnp.float32)).astype(jnp.bfloat16)


def product(left, right):
    return (
        jnp.dot(left[0], right[0], preferred_element_type=jnp.float32)
        + jnp.dot(left[1], right[0], preferred_element_type=jnp.float32)
        + jnp.dot(left[0], right[1], preferred_element_type=jnp.float32)
    )


def left_kernel(block, left):
    left[0], left[1] = halves(block[...].T)


def right_kernel(weight, block, right):
    columns = pl.ds(0, block.shape[1])
    right[0, :, columns], right[1, :, columns] = halves(block[...] * weight[...])


def ready_kernel(orders, weight, *refs):
    blocks, (far_left, xp_left, xp_right, zn_right) = refs[:3], refs[3:]
    even, x, c = place()
    for core, order in enumerate(orders):

        @pl.when(c == core)
        def _():
            left_kernel(blocks[order.index("far")], far_left)
            right_kernel(weight, blocks[order.index("zn")], zn_right)

            @pl.when(even | (x == 0))
            def _():
                left_kernel(blocks[order.index("xp")], xp_left)
                right_kernel(weight, blocks[order.index("xp")], xp_right)

            @pl.when(~even & (x == 1))
            def _():
                xp_left[...] = jnp.zeros_like(xp_left)
                xp_right[...] = jnp.zeros_like(xp_right)


def meet_kernel(far, xp, xp_scaled, zn_scaled, mine, theirs):
    even, x, c = place()
    rows = mine.shape[1]
    half = rows // 2
    scaled = [jnp.concatenate([zn_scaled[i], xp_scaled[i]], 1) for i in range(2)]
    by_far = product(far, scaled)
    far_zn, far_xp = by_far[:, :rows], by_far[:, 128 : 128 + rows]

    def put(core, row, values):
        @pl.when(c == core)
        def _():
            mine[pl.ds(row, values.shape[0]), :] = values

        @pl.when(c != core)
        def _():
            theirs[pl.ds(row, values.shape[0]), :] = values

    put(0, rows, far_zn[:half])
    put(1, rows, far_zn[half:])

    @pl.when(even)
    def _():
        zn_xp = product(xp, zn_scaled)[:, :rows].T
        put(1, 0, zn_xp)

        @pl.when(x == 0)
        def _():
            put(0, 0, far_xp)

        @pl.when(x == 1)
        def _():
            put(0, 0, zn_xp)

    @pl.when(~even)
    def _():
        zn_far = far_zn.T
        put(1, 0, zn_far)

        @pl.when(x == 0)
        def _():
            put(0, 0, far_xp)

        @pl.when(x == 1)
        def _():
            put(0, 0, zn_far)


def sum_kernel(mine, theirs, tile, half_tile):
    rows, half = tile.shape[0], half_tile.shape[0]
    tile[...] = mine[pl.ds(0, rows), :] + theirs[pl.ds(0, rows), :]
    half_tile[...] = mine[pl.ds(rows, half), :] + theirs[pl.ds(rows, half), :]


def own_kernel(own, own_scaled, own_own):
    own_own[...] = product(own, own_scaled)[:, : own_own.shape[1]]


def local_kernel(own, own_scaled, own_own, far, xp, zn_scaled, mine, theirs):
    _, _, c = place()
    rows = mine.shape[1]
    half = rows // 2
    far_own = product(far, own_scaled)[:, :rows]
    xp_own = product(xp, own_scaled)[:, :rows]
    zn_own = product(own, zn_scaled)[:, :rows].T

    def first(kept):
        kept[pl.ds(0, rows), :] = own_own[...]
        kept[pl.ds(rows, rows), :] = xp_own
        kept[pl.ds(2 * rows, half), :] = zn_own[:half]

    def second(kept):
        kept[pl.ds(0, half), :] = zn_own[half:]
        kept[pl.ds(half, rows), :] = jnp.zeros((rows, rows), jnp.float32)
        kept[pl.ds(half + rows, rows), :] = far_own

    @pl.when(c == 0)
    def _():
        first(mine)
        second(theirs)

    @pl.when(c == 1)
    def _():
        first(theirs)
        second(mine)


def finish_kernel(mine, theirs, tile, half_tile, response):
    even, x, c = place()
    rows = tile.shape[0]
    half = rows // 2
    response[...] = mine[...] + theirs[...]

    @pl.when((c == 0) & (x == 1))
    def _():
        response[pl.ds(rows, rows), :] = tile[...]

    @pl.when(c == 1)
    def _():
        response[pl.ds(half, rows), :] = tile[...]

    @pl.when((c == 0) & ~even)
    def _():
        response[pl.ds(2 * rows, half), :] = half_tile[...]

    @pl.when((c == 1) & ~even)
    def _():
        response[pl.ds(0, half), :] = half_tile[...]


def in_vmem(kernel, outs, *operands, flops=1000):
    whole = pl.BlockSpec(memory_space=pltpu.VMEM)
    return pl.pallas_call(
        kernel,
        out_shape=[jax.ShapeDtypeStruct(*out) for out in outs],
        in_specs=[whole] * len(operands),
        out_specs=[whole] * len(outs),
        compiler_params=pltpu.CompilerParams(vmem_limit_bytes=32 * 1024 * 1024),
        cost_estimate=pl.CostEstimate(flops=flops, bytes_accessed=1000, transcendentals=0),
    )(*operands)


def octet_shards(pair_tensor, occ_energy, vir_energy, frequency):
    own = pair_tensor.T
    pairs, rows = own.shape
    weight = jnp.broadcast_to(
        pair_weights(occ_energy, vir_energy, frequency)[:, None], (pairs, rows)
    )
    left, right = ((2, rows, pairs), jnp.bfloat16), ((2, pairs, 128), jnp.bfloat16)
    square, half_square = ((rows, rows), jnp.float32), ((rows // 2, rows), jnp.float32)
    routes = {"far": far_chip, "xp": other_x, "zn": next_chip}
    blocks = [
        sent(own, lambda z, x, c, slot=slot: routes[ORDERS[c][slot]](z, x, c)) for slot in range(3)
    ]
    far_left, xp_left, xp_right, zn_right = in_vmem(
        functools.partial(ready_kernel, ORDERS), [left, left, right, right], weight, *blocks
    )
    (own_left,) = in_vmem(left_kernel, [left], own)
    (own_right,) = in_vmem(right_kernel, [right], weight, own)
    (own_own,) = in_vmem(own_kernel, [square], own_left, own_right)
    parts = ((3 * rows // 2, rows), jnp.float32)
    mine, theirs = in_vmem(meet_kernel, [parts] * 2, far_left, xp_left, xp_right, zn_right)
    tile, half_tile = in_vmem(
        sum_kernel, [square, half_square], mine, sent(theirs, other_core)
    )
    tile = sent(tile, tile_chip)
    half_tile = sent(half_tile, half_tile_chip)
    kept = ((5 * rows // 2, rows), jnp.float32)
    mine, theirs = in_vmem(
        local_kernel, [kept] * 2, own_left, own_right, own_own, far_left, xp_left, zn_right
    )
    (response,) = in_vmem(
        finish_kernel, [kept], mine, sent(theirs, other_core), tile, half_tile
    )
    return response.T


def solution(mesh):
    in_specs = (P(("parts", "aux"), "pair"), P(("parts", "pair")), P("parts"), P("parts"))
    out_specs = P(("parts", "aux"), "pair")
    octet = mesh.shape["aux"] == 8 and mesh.shape["pair"] == 2
    shards = octet_shards if octet else ring_shards
    return jax.shard_map(shards, mesh=mesh, in_specs=in_specs, out_specs=out_specs, check_vma=False)
```

```python
import functools

import jax
import jax.numpy as jnp
from jax import lax
from jax.experimental import pallas as pl
from jax.experimental.pallas import tpu as pltpu
from jax.sharding import PartitionSpec as P


def passed_along(value, axis, by):
    peers = lax.axis_size(axis)
    return lax.ppermute(value, axis, [(i, (i + by) % peers) for i in range(peers)])


def pair_weights(occ_energy, vir_energy, frequency):
    energy_gap = vir_energy[None, :] - occ_energy[:, None]
    return (4.0 * energy_gap / (energy_gap * energy_gap + frequency[0] * frequency[0])).reshape(-1)


def product_tile(scaled_rows, block_rows):
    return lax.dot_general(
        scaled_rows,
        block_rows,
        (((1,), (1,)), ((), ())),
        precision=lax.Precision.HIGHEST,
        preferred_element_type=jnp.float32,
    )


def write_block(collected, values, column):
    return lax.dynamic_update_slice_in_dim(collected, values, column, 1)


def half_turn(scaled_rows, first_block, half_span):
    row_count = scaled_rows.shape[0]
    collected = jnp.zeros((row_count, (half_span + 1) * row_count), jnp.float32)
    collected = write_block(collected, product_tile(scaled_rows, first_block), 0)
    opposite = passed_along(first_block, "aux", -half_span)
    collected = write_block(collected, product_tile(scaled_rows, opposite), half_span * row_count)

    def advance(turn_index, loop_state):
        collected, forward, backward = loop_state
        forward = passed_along(forward, "aux", -1)
        backward = passed_along(backward, "aux", 1)
        collected = write_block(
            collected, product_tile(scaled_rows, forward), turn_index * row_count
        )
        collected = write_block(
            collected, product_tile(scaled_rows, backward), (half_span - turn_index) * row_count
        )
        return (collected, forward, backward)

    collected, forward, backward = lax.fori_loop(
        1, half_span // 2, advance, (collected, first_block, opposite)
    )
    middle = passed_along(forward, "aux", -1)
    return write_block(collected, product_tile(scaled_rows, middle), half_span // 2 * row_count)


def ring_shards(pair_tensor, occ_energy, vir_energy, frequency):
    n_aux = lax.axis_size("aux")
    scaled_rows = pair_tensor * pair_weights(occ_energy, vir_energy, frequency)[None, :]
    collected = half_turn(scaled_rows, pair_tensor, n_aux // 2)
    return lax.psum_scatter(collected, "pair", scatter_dimension=1, tiled=True)


def sent(value, target_of):
    pairs = []
    for z in range(4):
        for x in range(2):
            for c in range(2):
                tz, tx, tc = target_of(z, x, c)
                pairs.append(((z * 2 + x) * 2 + c, (tz * 2 + tx) * 2 + tc))
    return lax.ppermute(value, ("aux", "pair"), pairs)


def other_core(z, x, c):
    return (z, x, 1 - c)


ORDERS = (("zn", "xp", "far"), ("far", "zn", "xp"))


def far_chip(z, x, c):
    return (z ^ 2, x, c)


def other_x(z, x, c):
    return (z, 1 - x, c)


def next_chip(z, x, c):
    return (z ^ 1, x if z % 2 else 1 - x, c)


def tile_chip(z, x, c):
    return (z ^ 2, x, c) if z % 2 and x != c else (z, 1 - x, 1 - c)


def half_tile_chip(z, x, c):
    return (z ^ 1, x, c)


def place():
    block = lax.axis_index("aux")
    return lax.rem(block // 2, 2) == 0, lax.rem(block, 2), lax.axis_index("pair")


def halves(value):
    high = value.astype(jnp.bfloat16)
    return high, (value - high.astype(jnp.float32)).astype(jnp.bfloat16)


def product(left, right):
    return (
        jnp.dot(left[0], right[0], preferred_element_type=jnp.float32)
        + jnp.dot(left[1], right[0], preferred_element_type=jnp.float32)
        + jnp.dot(left[0], right[1], preferred_element_type=jnp.float32)
    )


def left_kernel(block, left):
    left[0], left[1] = halves(block[...].T)


def right_kernel(weight, block, right):
    columns = pl.ds(0, block.shape[1])
    right[0, :, columns], right[1, :, columns] = halves(block[...] * weight[...])


def ready_kernel(orders, weight, *refs):
    blocks, (far_left, xp_left, xp_right, zn_right) = refs[:3], refs[3:]
    even, x, c = place()
    for core, order in enumerate(orders):

        @pl.when(c == core)
        def _():
            left_kernel(blocks[order.index("far")], far_left)
            right_kernel(weight, blocks[order.index("zn")], zn_right)

            @pl.when(even | (x == 0))
            def _():
                left_kernel(blocks[order.index("xp")], xp_left)
                right_kernel(weight, blocks[order.index("xp")], xp_right)

            @pl.when(~even & (x == 1))
            def _():
                xp_left[...] = jnp.zeros_like(xp_left)
                xp_right[...] = jnp.zeros_like(xp_right)


def meet_kernel(far, xp, xp_scaled, zn_scaled, mine, theirs, by_far):
    even, x, c = place()
    rows = mine.shape[1]
    half = rows // 2
    @pl.when(x == 0)
    def _():
        scaled = [jnp.concatenate([zn_scaled[i], xp_scaled[i]], 1) for i in range(2)]
        by_far[...] = product(far, scaled)

    @pl.when(x == 1)
    def _():
        by_far[:, pl.ds(0, 128)] = product(far, zn_scaled)

    far_zn = by_far[:, pl.ds(0, rows)]

    def put(core, row, values):
        @pl.when(c == core)
        def _():
            mine[pl.ds(row, values.shape[0]), :] = values

        @pl.when(c != core)
        def _():
            theirs[pl.ds(row, values.shape[0]), :] = values

    put(0, rows, far_zn[:half])
    put(1, rows, far_zn[half:])

    @pl.when(even)
    def _():
        zn_xp = product(xp, zn_scaled)[:, :rows].T
        put(1, 0, zn_xp)

        @pl.when(x == 0)
        def _():
            put(0, 0, by_far[:, pl.ds(128, rows)])

        @pl.when(x == 1)
        def _():
            put(0, 0, zn_xp)

    @pl.when(~even)
    def _():
        zn_far = far_zn.T
        put(1, 0, zn_far)

        @pl.when(x == 0)
        def _():
            put(0, 0, by_far[:, pl.ds(128, rows)])

        @pl.when(x == 1)
        def _():
            put(0, 0, zn_far)


def sum_kernel(mine, theirs, tile, half_tile):
    rows, half = tile.shape[0], half_tile.shape[0]
    tile[...] = mine[pl.ds(0, rows), :] + theirs[pl.ds(0, rows), :]
    half_tile[...] = mine[pl.ds(rows, half), :] + theirs[pl.ds(rows, half), :]


def own_kernel(own, own_scaled, own_own):
    own_own[...] = product(own, own_scaled)[:, : own_own.shape[1]]


def local_kernel(own, own_scaled, own_own, far, xp, zn_scaled, mine, theirs):
    _, _, c = place()
    rows = mine.shape[1]
    half = rows // 2
    far_own = product(far, own_scaled)[:, :rows]
    xp_own = product(xp, own_scaled)[:, :rows]
    zn_own = product(own, zn_scaled)[:, :rows].T

    def first(kept):
        kept[pl.ds(0, rows), :] = own_own[...]
        kept[pl.ds(rows, rows), :] = xp_own
        kept[pl.ds(2 * rows, half), :] = zn_own[:half]

    def second(kept):
        kept[pl.ds(0, half), :] = zn_own[half:]
        kept[pl.ds(half, rows), :] = jnp.zeros((rows, rows), jnp.float32)
        kept[pl.ds(half + rows, rows), :] = far_own

    @pl.when(c == 0)
    def _():
        first(mine)
        second(theirs)

    @pl.when(c == 1)
    def _():
        first(theirs)
        second(mine)


def finish_kernel(mine, theirs, tile, half_tile, response):
    even, x, c = place()
    rows = tile.shape[0]
    half = rows // 2
    response[...] = mine[...] + theirs[...]

    @pl.when((c == 0) & (x == 1))
    def _():
        response[pl.ds(rows, rows), :] = tile[...]

    @pl.when(c == 1)
    def _():
        response[pl.ds(half, rows), :] = tile[...]

    @pl.when((c == 0) & ~even)
    def _():
        response[pl.ds(2 * rows, half), :] = half_tile[...]

    @pl.when((c == 1) & ~even)
    def _():
        response[pl.ds(0, half), :] = half_tile[...]


def in_vmem(kernel, outs, *operands, scratch=()):
    whole = pl.BlockSpec(memory_space=pltpu.VMEM)
    return pl.pallas_call(
        kernel,
        out_shape=[jax.ShapeDtypeStruct(*out) for out in outs],
        in_specs=[whole] * len(operands),
        out_specs=[whole] * len(outs),
        scratch_shapes=[pltpu.VMEM(shape, jnp.float32) for shape in scratch],
        compiler_params=pltpu.CompilerParams(vmem_limit_bytes=32 * 1024 * 1024),
        cost_estimate=pl.CostEstimate(flops=1000, bytes_accessed=1000, transcendentals=0),
    )(*operands)


def octet_shards(pair_tensor, occ_energy, vir_energy, frequency):
    own = pair_tensor.T
    pairs, rows = own.shape
    weight = jnp.broadcast_to(
        pair_weights(occ_energy, vir_energy, frequency)[:, None], (pairs, rows)
    )
    left, right = ((2, rows, pairs), jnp.bfloat16), ((2, pairs, 128), jnp.bfloat16)
    square, half_square = ((rows, rows), jnp.float32), ((rows // 2, rows), jnp.float32)
    routes = {"far": far_chip, "xp": other_x, "zn": next_chip}
    blocks = [
        sent(own, lambda z, x, c, slot=slot: routes[ORDERS[c][slot]](z, x, c)) for slot in range(3)
    ]
    far_left, xp_left, xp_right, zn_right = in_vmem(
        functools.partial(ready_kernel, ORDERS), [left, left, right, right], weight, *blocks
    )
    (own_left,) = in_vmem(left_kernel, [left], own)
    (own_right,) = in_vmem(right_kernel, [right], weight, own)
    (own_own,) = in_vmem(own_kernel, [square], own_left, own_right)
    parts = ((3 * rows // 2, rows), jnp.float32)
    mine, theirs = in_vmem(
        meet_kernel,
        [parts] * 2,
        far_left,
        xp_left,
        xp_right,
        zn_right,
        scratch=[(rows, 256)],
    )
    tile, half_tile = in_vmem(
        sum_kernel, [square, half_square], mine, sent(theirs, other_core)
    )
    tile = sent(tile, tile_chip)
    half_tile = sent(half_tile, half_tile_chip)
    kept = ((5 * rows // 2, rows), jnp.float32)
    mine, theirs = in_vmem(
        local_kernel, [kept] * 2, own_left, own_right, own_own, far_left, xp_left, zn_right
    )
    (response,) = in_vmem(
        finish_kernel, [kept], mine, sent(theirs, other_core), tile, half_tile
    )
    return response.T


def solution(mesh):
    in_specs = (P(("parts", "aux"), "pair"), P(("parts", "pair")), P("parts"), P("parts"))
    out_specs = P(("parts", "aux"), "pair")
    octet = mesh.shape["aux"] == 8 and mesh.shape["pair"] == 2
    shards = octet_shards if octet else ring_shards
    return jax.shard_map(shards, mesh=mesh, in_specs=in_specs, out_specs=out_specs, check_vma=False)
```

```python
import functools

import jax
import jax.numpy as jnp
from jax import lax
from jax.experimental import pallas as pl
from jax.experimental.pallas import tpu as pltpu
from jax.sharding import PartitionSpec as P


def passed_along(value, axis, by):
    peers = lax.axis_size(axis)
    return lax.ppermute(value, axis, [(i, (i + by) % peers) for i in range(peers)])


def pair_weights(occ_energy, vir_energy, frequency):
    energy_gap = vir_energy[None, :] - occ_energy[:, None]
    return (4.0 * energy_gap / (energy_gap * energy_gap + frequency[0] * frequency[0])).reshape(-1)


def product_tile(scaled_rows, block_rows):
    return lax.dot_general(
        scaled_rows,
        block_rows,
        (((1,), (1,)), ((), ())),
        precision=lax.Precision.HIGHEST,
        preferred_element_type=jnp.float32,
    )


def write_block(collected, values, column):
    return lax.dynamic_update_slice_in_dim(collected, values, column, 1)


def half_turn(scaled_rows, first_block, half_span):
    row_count = scaled_rows.shape[0]
    collected = jnp.zeros((row_count, (half_span + 1) * row_count), jnp.float32)
    collected = write_block(collected, product_tile(scaled_rows, first_block), 0)
    opposite = passed_along(first_block, "aux", -half_span)
    collected = write_block(collected, product_tile(scaled_rows, opposite), half_span * row_count)

    def advance(turn_index, loop_state):
        collected, forward, backward = loop_state
        forward = passed_along(forward, "aux", -1)
        backward = passed_along(backward, "aux", 1)
        collected = write_block(
            collected, product_tile(scaled_rows, forward), turn_index * row_count
        )
        collected = write_block(
            collected, product_tile(scaled_rows, backward), (half_span - turn_index) * row_count
        )
        return (collected, forward, backward)

    collected, forward, backward = lax.fori_loop(
        1, half_span // 2, advance, (collected, first_block, opposite)
    )
    middle = passed_along(forward, "aux", -1)
    return write_block(collected, product_tile(scaled_rows, middle), half_span // 2 * row_count)


def ring_shards(pair_tensor, occ_energy, vir_energy, frequency):
    n_aux = lax.axis_size("aux")
    scaled_rows = pair_tensor * pair_weights(occ_energy, vir_energy, frequency)[None, :]
    collected = half_turn(scaled_rows, pair_tensor, n_aux // 2)
    return lax.psum_scatter(collected, "pair", scatter_dimension=1, tiled=True)


def sent(value, target_of):
    pairs = []
    for z in range(4):
        for x in range(2):
            for c in range(2):
                tz, tx, tc = target_of(z, x, c)
                pairs.append(((z * 2 + x) * 2 + c, (tz * 2 + tx) * 2 + tc))
    return lax.ppermute(value, ("aux", "pair"), pairs)


def other_core(z, x, c):
    return (z, x, 1 - c)


ORDERS = (("far", "xp", "zn"), ("xp", "zn", "far"))


def far_chip(z, x, c):
    return (z ^ 2, x, c)


def other_x(z, x, c):
    return (z, 1 - x, c)


def next_chip(z, x, c):
    return (z ^ 1, x if z % 2 else 1 - x, c)


def tile_chip(z, x, c):
    return (z ^ 2, x, c) if z % 2 and x != c else (z, 1 - x, 1 - c)


def half_tile_chip(z, x, c):
    return (z ^ 1, x, c)


def place():
    block = lax.axis_index("aux")
    return lax.rem(block // 2, 2) == 0, lax.rem(block, 2), lax.axis_index("pair")


def halves(value):
    high = value.astype(jnp.bfloat16)
    return high, (value - high.astype(jnp.float32)).astype(jnp.bfloat16)


def product(left, right):
    return (
        jnp.dot(left[0], right[0], preferred_element_type=jnp.float32)
        + jnp.dot(left[1], right[0], preferred_element_type=jnp.float32)
        + jnp.dot(left[0], right[1], preferred_element_type=jnp.float32)
    )


def left_kernel(block, left):
    left[0], left[1] = halves(block[...].T)


def right_kernel(weight, block, right):
    columns = pl.ds(0, block.shape[1])
    right[0, :, columns], right[1, :, columns] = halves(block[...] * weight[...])


def ready_kernel(orders, weight, *refs):
    blocks, (far_left, xp_left, xp_right, zn_right) = refs[:3], refs[3:]
    even, x, c = place()
    for core, order in enumerate(orders):

        @pl.when(c == core)
        def _():
            left_kernel(blocks[order.index("far")], far_left)
            right_kernel(weight, blocks[order.index("zn")], zn_right)

            @pl.when(even | (x == 0))
            def _():
                left_kernel(blocks[order.index("xp")], xp_left)
                right_kernel(weight, blocks[order.index("xp")], xp_right)

            @pl.when(~even & (x == 1))
            def _():
                xp_left[...] = jnp.zeros_like(xp_left)
                xp_right[...] = jnp.zeros_like(xp_right)


def meet_kernel(far, xp, xp_scaled, zn_scaled, mine, theirs):
    even, x, c = place()
    rows = mine.shape[1]
    half = rows // 2
    scaled = [jnp.concatenate([zn_scaled[i], xp_scaled[i]], 1) for i in range(2)]
    by_far = product(far, scaled)
    far_zn, far_xp = by_far[:, :rows], by_far[:, 128 : 128 + rows]

    def put(core, row, values):
        @pl.when(c == core)
        def _():
            mine[pl.ds(row, values.shape[0]), :] = values

        @pl.when(c != core)
        def _():
            theirs[pl.ds(row, values.shape[0]), :] = values

    put(0, rows, far_zn[:half])
    put(1, rows, far_zn[half:])

    @pl.when(even)
    def _():
        zn_xp = product(xp, zn_scaled)[:, :rows].T
        put(1, 0, zn_xp)

        @pl.when(x == 0)
        def _():
            put(0, 0, far_xp)

        @pl.when(x == 1)
        def _():
            put(0, 0, zn_xp)

    @pl.when(~even)
    def _():
        zn_far = far_zn.T
        put(1, 0, zn_far)

        @pl.when(x == 0)
        def _():
            put(0, 0, far_xp)

        @pl.when(x == 1)
        def _():
            put(0, 0, zn_far)


def sum_kernel(mine, theirs, tile, half_tile):
    rows, half = tile.shape[0], half_tile.shape[0]
    tile[...] = mine[pl.ds(0, rows), :] + theirs[pl.ds(0, rows), :]
    half_tile[...] = mine[pl.ds(rows, half), :] + theirs[pl.ds(rows, half), :]


def own_kernel(own, own_scaled, own_own):
    own_own[...] = product(own, own_scaled)[:, : own_own.shape[1]]


def local_kernel(own, own_scaled, own_own, far, xp, zn_scaled, mine, theirs):
    _, _, c = place()
    rows = mine.shape[1]
    half = rows // 2
    far_own = product(far, own_scaled)[:, :rows]
    xp_own = product(xp, own_scaled)[:, :rows]
    zn_own = product(own, zn_scaled)[:, :rows].T

    def first(kept):
        kept[pl.ds(0, rows), :] = own_own[...]
        kept[pl.ds(rows, rows), :] = xp_own
        kept[pl.ds(2 * rows, half), :] = zn_own[:half]

    def second(kept):
        kept[pl.ds(0, half), :] = zn_own[half:]
        kept[pl.ds(half, rows), :] = jnp.zeros((rows, rows), jnp.float32)
        kept[pl.ds(half + rows, rows), :] = far_own

    @pl.when(c == 0)
    def _():
        first(mine)
        second(theirs)

    @pl.when(c == 1)
    def _():
        first(theirs)
        second(mine)


def finish_kernel(mine, theirs, tile, half_tile, response):
    even, x, c = place()
    rows = tile.shape[0]
    half = rows // 2
    response[...] = mine[...] + theirs[...]

    @pl.when((c == 0) & (x == 1))
    def _():
        response[pl.ds(rows, rows), :] = tile[...]

    @pl.when(c == 1)
    def _():
        response[pl.ds(half, rows), :] = tile[...]

    @pl.when((c == 0) & ~even)
    def _():
        response[pl.ds(2 * rows, half), :] = half_tile[...]

    @pl.when((c == 1) & ~even)
    def _():
        response[pl.ds(0, half), :] = half_tile[...]


def in_vmem(kernel, outs, *operands, flops=1000):
    whole = pl.BlockSpec(memory_space=pltpu.VMEM)
    return pl.pallas_call(
        kernel,
        out_shape=[jax.ShapeDtypeStruct(*out) for out in outs],
        in_specs=[whole] * len(operands),
        out_specs=[whole] * len(outs),
        compiler_params=pltpu.CompilerParams(vmem_limit_bytes=32 * 1024 * 1024),
        cost_estimate=pl.CostEstimate(flops=flops, bytes_accessed=1000, transcendentals=0),
    )(*operands)


def octet_shards(pair_tensor, occ_energy, vir_energy, frequency):
    own = pair_tensor.T
    pairs, rows = own.shape
    weight = jnp.broadcast_to(
        pair_weights(occ_energy, vir_energy, frequency)[:, None], (pairs, rows)
    )
    left, right = ((2, rows, pairs), jnp.bfloat16), ((2, pairs, 128), jnp.bfloat16)
    square, half_square = ((rows, rows), jnp.float32), ((rows // 2, rows), jnp.float32)
    routes = {"far": far_chip, "xp": other_x, "zn": next_chip}
    blocks = [
        sent(own, lambda z, x, c, slot=slot: routes[ORDERS[c][slot]](z, x, c)) for slot in range(3)
    ]
    (own_left,) = in_vmem(left_kernel, [left], own)
    (own_right,) = in_vmem(right_kernel, [right], weight, own)
    (own_own,) = in_vmem(own_kernel, [square], own_left, own_right)
    weight, own_own = lax.optimization_barrier((weight, own_own))
    far_left, xp_left, xp_right, zn_right = in_vmem(
        functools.partial(ready_kernel, ORDERS), [left, left, right, right], weight, *blocks
    )
    parts = ((3 * rows // 2, rows), jnp.float32)
    mine, theirs = in_vmem(meet_kernel, [parts] * 2, far_left, xp_left, xp_right, zn_right)
    tile, half_tile = in_vmem(
        sum_kernel, [square, half_square], mine, sent(theirs, other_core)
    )
    tile = sent(tile, tile_chip)
    half_tile = sent(half_tile, half_tile_chip)
    kept = ((5 * rows // 2, rows), jnp.float32)
    mine, theirs = in_vmem(
        local_kernel, [kept] * 2, own_left, own_right, own_own, far_left, xp_left, zn_right
    )
    (response,) = in_vmem(
        finish_kernel, [kept], mine, sent(theirs, other_core), tile, half_tile
    )
    return response.T


def solution(mesh):
    in_specs = (P(("parts", "aux"), "pair"), P(("parts", "pair")), P("parts"), P("parts"))
    out_specs = P(("parts", "aux"), "pair")
    octet = mesh.shape["aux"] == 8 and mesh.shape["pair"] == 2
    shards = octet_shards if octet else ring_shards
    return jax.shard_map(shards, mesh=mesh, in_specs=in_specs, out_specs=out_specs, check_vma=False)
```
